32 devices in a mesh: grp: 2 (over x), tile: 16 (over z, y, core).
Axes of the slice: x: 2, y: 2, z: 4, core: 2. Of those that a mesh axis runs over, the one named last changes fastest.
Arguments:
- ocean_state: float32 [3, 24, 256, 4096], P(None, None, 'tile', 'grp'), may hold values from -6 to 6
- biharmonic: float32 [256, 4096], P('tile', 'grp'), may hold values from 0.004 to 0.014
- prev_stress: float32 [2, 256, 4096], P(None, 'tile', 'grp'), may hold values from -4 to 4
- ice_state: float32 [5, 256, 4096], P(None, 'tile', 'grp'), may hold values from -2 to 2
- strength: float32 [256, 4096], P('tile', 'grp'), may hold values from 0.5 to 2
- ice_mass: float32 [256, 4096], P('tile', 'grp'), may hold values from 0.5 to 2
- ice_fraction: float32 [256, 4096], P('tile', 'grp'), may hold values from 0.15 to 1
- wind_stress: float32 [2, 256, 4096], P(None, 'tile', 'grp'), may hold values from -2 to 2
- ice_count: int32 [32], P(('grp', 'tile')), may hold values from 0 to 16, as said below
- ice_list: int32 [32, 16], P(('grp', 'tile')), may hold values from 0 to 15, as said below
Outputs:
- ocean_out: float32 [3, 24, 256, 4096], P(None, None, 'tile', 'grp')
- ice_out: float32 [5, 256, 4096], P(None, 'tile', 'grp')
- stress_out: float32 [2, 256, 4096], P(None, 'tile', 'grp')
The draws below stay inside these ranges and needn't reach their ends.
Inputs may be any that keep to these rules, and one draw needn't show every extreme that they name: `ice_count`: the tiles g * 16 + t and g * 16 + (t + 16 / 2) % 16 together have at most 16 ice-covered blocks, and some such pair has exactly 16; tiles near the first and last rows have the most. `ice_list`: each row is an ordering of the tile's 16 block numbers.
All inputs are finite; a program needn't handle non-finite values.
Results may differ from the reference program's by a relative error of at most 0.00002.
Values sent between devices are 32-bit elements; how exact they have to be, the bound alone decides.
No kernel may reach another device: no remote copies, remote signals or barrier semaphores. Data moves between devices by JAX's collectives and lax.ppermute only.
A program may use at most 192 MiB of HBM per device.

```python
import math
import jax
import jax.numpy as jnp
from jax import lax

LEV = 24
CY = 16
CX = 2048
BY = 16
BX = 128
SUBCYCLES = 64
NY = 256
NX = 4096
OWNERS = 32
NB_DEV = 16
N_GRP = 2
N_TILE = 16


def ice_layout(key):
    quarter = N_TILE // 4
    halfway = N_TILE // 2
    base = jnp.arange(halfway, dtype=jnp.int32)
    polar = jnp.minimum(base, halfway - 1 - base)
    spread = 1 + polar * (NB_DEV // 2) // quarter
    first_key, second_key = jax.random.split(jax.random.fold_in(key, 11))
    reduction = jax.random.randint(first_key, (N_GRP, halfway), 0, spread[None, :])
    heavy = NB_DEV - reduction
    light = jax.random.randint(second_key, (N_GRP, halfway), 0, NB_DEV - heavy + 1)
    first_heavy = (base < quarter)[None, :]
    first = jnp.where(first_heavy, heavy, light)
    second = jnp.where(first_heavy, light, heavy)
    return jnp.concatenate([first, second], axis=1).reshape(N_GRP * N_TILE).astype(jnp.int32)


def draw_ice_count(key, part):
    return ice_layout(key)


def draw_ice_list(key, part):
    scores = jax.random.randint(jax.random.fold_in(key, 23), (OWNERS, NB_DEV), 0, 1 << 20)
    scores = scores * NB_DEV + jnp.arange(NB_DEV, dtype=jnp.int32)[None, :]
    return jnp.argsort(scores, axis=1).astype(jnp.int32)


def shard_levels(stream_key, extent, shards, least, largest):
    level = 1.0
    for dim, parts in shards:
        draws = jax.random.uniform(jax.random.fold_in(jax.random.fold_in(stream_key, 6), dim), (parts,), jnp.float32, least / len(shards), largest / len(shards))
        level = level * jnp.repeat(jnp.exp(draws), extent[dim] // parts).reshape((-1,) + (1,) * (len(extent) - 1 - dim))
    return level


def scatter_about(rng, dims, scale, bound, cuts=(), kind=jnp.bfloat16):
    factor_of = shard_levels(rng, dims, cuts, -0.22, 0.18) if cuts else 1.0
    drawn = jax.random.normal(rng, dims, jnp.float32) * scale * factor_of
    return jnp.minimum(jnp.maximum(drawn, -bound), bound).astype(kind)


def setup_inputs(seed: int = 0) -> dict:
    streams_of = jax.random.split(jax.random.key(seed), 11)
    return {
        "ocean_state": scatter_about(streams_of[0], (3, LEV, NY, NX), 1.0, 6.0, ((2, 16), (3, 2)), jnp.float32),
        "biharmonic": jnp.clip(jnp.exp(math.log(0.014) - 1.25276295 * jax.random.uniform(streams_of[1], (NY, NX), jnp.float32) ** shard_levels(streams_of[1], (NY, NX), ((0, 16), (1, 2)), -0.2, 0.2)), 0.004, 0.014),
        "prev_stress": scatter_about(streams_of[2], (2, NY, NX), 0.5, 4.0, ((1, 16), (2, 2)), jnp.float32),
        "ice_state": scatter_about(streams_of[3], (5, NY, NX), 0.3, 2.0, ((1, 16), (2, 2)), jnp.float32),
        "strength": jnp.clip(jnp.exp(math.log(2.0) - 1.3862944 * jax.random.uniform(streams_of[4], (NY, NX), jnp.float32) ** shard_levels(streams_of[4], (NY, NX), ((0, 16), (1, 2)), -0.2, 0.2)), 0.5, 2.0),
        "ice_mass": jnp.clip(jnp.exp(math.log(2.0) - 1.3862944 * jax.random.uniform(streams_of[5], (NY, NX), jnp.float32) ** shard_levels(streams_of[5], (NY, NX), ((0, 16), (1, 2)), -0.2, 0.2)), 0.5, 2.0),
        "ice_fraction": jnp.clip(0.15 + 0.85 * jax.random.uniform(streams_of[6], (NY, NX), jnp.float32) ** shard_levels(streams_of[6], (NY, NX), ((0, 16), (1, 2)), -0.2, 0.2), 0.15, 1.0),
        "wind_stress": scatter_about(streams_of[7], (2, NY, NX), 0.3, 2.0, ((1, 16), (2, 2)), jnp.float32),
        "ice_count": draw_ice_count(jax.random.fold_in(streams_of[10], 71), 0),
        "ice_list": draw_ice_list(jax.random.fold_in(streams_of[10], 71), 0),
    }


kv_mix = 0.2
relax_rate = 0.5
sub_step = 0.3
drag_coef = 1.0
turning = 0.3
delta_min = 0.5
coriolis_scale = 0.2

def ahead_diff(field, axis):
    length = field.shape[axis]
    inner = lax.slice_in_dim(field, 1, length, axis=axis) - lax.slice_in_dim(field, 0, length - 1, axis=axis)
    return jnp.concatenate([inner, jnp.zeros_like(lax.slice_in_dim(field, 0, 1, axis=axis))], axis=axis)

def behind_diff(field, axis):
    length = field.shape[axis]
    inner = lax.slice_in_dim(field, 1, length, axis=axis) - lax.slice_in_dim(field, 0, length - 1, axis=axis)
    return jnp.concatenate([lax.slice_in_dim(field, 0, 1, axis=axis), inner], axis=axis)

def ice_dynamics(fields, y_axis, x_axis):
    vel_x, vel_y, stress_xx, stress_yy, stress_xy, ice_strength, mass, fraction, wind_x, wind_y, ocean_x, ocean_y = fields
    pressure = relax_rate * ice_strength
    inertia = mass + sub_step * drag_coef

    def subcycle(step_index, carry):
        vel_x, vel_y, stress_xx, stress_yy, stress_xy = carry
        du_dx = ahead_diff(vel_x, x_axis)
        du_dy = ahead_diff(vel_x, y_axis)
        dv_dx = ahead_diff(vel_y, x_axis)
        dv_dy = ahead_diff(vel_y, y_axis)
        divergence = du_dx + dv_dy
        tension = du_dx - dv_dy
        shearing = du_dy + dv_dx
        deform = jnp.sqrt(divergence * divergence + 0.25 * (tension * tension + shearing * shearing) + delta_min * delta_min)
        sigma_one = (stress_xx + stress_yy + pressure * (divergence / deform - 1.0)) / (1.0 + relax_rate)
        sigma_two = (stress_xx - stress_yy + 0.25 * pressure * tension / deform) / (1.0 + relax_rate)
        stress_xy = (stress_xy + 0.125 * pressure * shearing / deform) / (1.0 + relax_rate)
        stress_xx = 0.5 * (sigma_one + sigma_two)
        stress_yy = 0.5 * (sigma_one - sigma_two)
        force_x = behind_diff(stress_xx, x_axis) + behind_diff(stress_xy, y_axis)
        force_y = behind_diff(stress_xy, x_axis) + behind_diff(stress_yy, y_axis)
        new_x = (mass * vel_x + sub_step * (force_x + wind_x + drag_coef * ocean_x + turning * mass * vel_y)) / inertia
        new_y = (mass * vel_y + sub_step * (force_y + wind_y + drag_coef * ocean_y - turning * mass * vel_x)) / inertia
        return (new_x, new_y, stress_xx, stress_yy, stress_xy)
    vel_x, vel_y, stress_xx, stress_yy, stress_xy = lax.fori_loop(0, SUBCYCLES, subcycle, (vel_x, vel_y, stress_xx, stress_yy, stress_xy))
    drag_x = fraction * drag_coef * (vel_x - ocean_x) + (1.0 - fraction) * wind_x
    drag_y = fraction * drag_coef * (vel_y - ocean_y) + (1.0 - fraction) * wind_y
    return (vel_x, vel_y, stress_xx, stress_yy, stress_xy, drag_x, drag_y)

def laplace(padded):
    return padded[..., 1:-1, 2:] + padded[..., 1:-1, :-2] + padded[..., 2:, 1:-1] + padded[..., :-2, 1:-1] - 4.0 * padded[..., 1:-1, 1:-1]

def vertical(field):
    upper = jnp.concatenate([field[:1], field[:-1]], axis=0)
    lower = jnp.concatenate([field[1:], field[-1:]], axis=0)
    return upper + lower - 2.0 * field

def ocean_field(padded, field, biharmonic):
    return field - biharmonic * laplace(laplace(padded)) + kv_mix * vertical(field)

def pad_ocean(field):
    padded = jnp.pad(field, ((0, 0), (2, 2), (0, 0)))
    return jnp.concatenate([padded[..., -2:], padded, padded[..., :2]], axis=-1)

def reference(ocean_state, biharmonic, prev_stress, ice_state, strength, ice_mass, ice_fraction, wind_stress, ice_count, ice_list):
    rows = jnp.arange(NY).astype(jnp.float32) + 0.5
    coriolis = (coriolis_scale * (2.0 * rows / NY - 1.0))[:, None]
    mixed = [ocean_field(pad_ocean(ocean_state[index]), ocean_state[index], biharmonic) for index in range(3)]
    east = mixed[0] + coriolis * ocean_state[1]
    north = mixed[1] - coriolis * ocean_state[0]
    east = east.at[0].add(prev_stress[0])
    north = north.at[0].add(prev_stress[1])
    ocean_out = jnp.stack([east, north, mixed[2]])
    row_blocks = NY // BY
    col_blocks = NX // BX
    grids = [ice_state[0], ice_state[1], ice_state[2], ice_state[3], ice_state[4], strength, ice_mass, ice_fraction, wind_stress[0], wind_stress[1], ocean_state[0, 0], ocean_state[1, 0]]
    fields = [grid.reshape(row_blocks, BY, col_blocks, BX) for grid in grids]
    results = ice_dynamics(fields, 1, 3)
    slots = jnp.arange(NB_DEV, dtype=jnp.int32)
    matches = ice_list[:, :, None] == slots[None, None, :]
    position = lax.optimization_barrier(jnp.sum(jnp.where(matches, slots[None, :, None], 0), axis=1))
    covered = position < ice_count[:, None]
    covered = covered.reshape(N_GRP, N_TILE, CY // BY, CX // BX).transpose(1, 2, 0, 3).reshape(row_blocks, col_blocks)
    covered = covered[:, None, :, None]
    ice_out = jnp.stack([jnp.where(covered, results[index], fields[index]).reshape(NY, NX) for index in range(5)])
    stress_out = jnp.stack([jnp.where(covered, results[5], fields[8]).reshape(NY, NX), jnp.where(covered, results[6], fields[9]).reshape(NY, NX)])
    return (ocean_out, ice_out, stress_out)
```

```python
import jax
import jax.numpy as jnp
from jax import lax
from jax.experimental import pallas as pl
from jax.experimental.pallas import tpu as pltpu
from jax.sharding import PartitionSpec as P

BY = 16
BX = 128
SUBCYCLES = 64
UNROLL = 4
LANES = 128
HALF = 8

KV_MIX = 0.2
RELAX = 0.5
SUB_STEP = 0.3
TURNING = 0.3
CORIOLIS = 0.2

DECAY = 1.0 / (1.0 + RELAX)
VMEM_BYTES = 48 * 1024 * 1024

HBM = pltpu.HBM
VMEM = pltpu.VMEM
SMEM = pltpu.SMEM


def spec(space):
    return pl.BlockSpec(memory_space=space)


def cost(flops, nbytes):
    return pl.CostEstimate(flops=flops, bytes_accessed=nbytes, transcendentals=0)


def lane_index(rows):
    return lax.broadcasted_iota(jnp.int32, (rows, LANES), 1)


def pack_kernel(x, first, last, cols, corners, left, right, cleft, cright, row_sem, col_sem):
    fields, levels, rows, width = x.shape
    edge_rows = (0, rows - 1)
    copies = []
    col_copies = [
        pltpu.make_async_copy(x.at[:, :, :, 0:LANES], left, col_sem.at[0]),
        pltpu.make_async_copy(x.at[:, :, :, width - LANES : width], right, col_sem.at[1]),
    ]
    for f in range(fields):
        for j in range(2):
            index = f * 2 + j
            copies.append(
                pltpu.make_async_copy(x.at[f, :, j, :], first.at[f, j], row_sem.at[0, index])
            )
            copies.append(
                pltpu.make_async_copy(
                    x.at[f, :, rows - 2 + j, :], last.at[f, j], row_sem.at[1, index]
                )
            )
            row = edge_rows[j]
            col_copies.append(
                pltpu.make_async_copy(
                    x.at[f, :, row, 0:LANES], cleft.at[j, f], col_sem.at[2 + 2 * index]
                )
            )
            col_copies.append(
                pltpu.make_async_copy(
                    x.at[f, :, row, width - LANES : width],
                    cright.at[j, f],
                    col_sem.at[3 + 2 * index],
                )
            )
    for copy in copies + col_copies:
        copy.start()
    for copy in col_copies:
        copy.wait()
    lane = lane_index(rows)
    for f in range(fields):
        packed = jnp.zeros((rows, LANES), jnp.float32)
        for k in range(levels):
            edge = jnp.where(lane < LANES // 2, left[f, k], right[f, k])
            if k:
                edge = pltpu.roll(edge, 4 * k, axis=1)
            mine = ((lane + (2 - 4 * k)) & (LANES - 1)) < 4
            packed = jnp.where(mine, edge, packed)
        cols[f] = packed
        for j in range(2):
            corners[j, f] = jnp.where(
                lane_index(levels) < LANES // 2, cleft[j, f], cright[j, f]
            )
    for copy in copies:
        copy.wait()


def pack(ocean_state):
    fields, levels, rows, width = ocean_state.shape
    f32 = jnp.float32
    return pl.pallas_call(
        pack_kernel,
        name="pack_edges",
        out_shape=(
            jax.ShapeDtypeStruct((fields, 2, levels, width), f32),
            jax.ShapeDtypeStruct((fields, 2, levels, width), f32),
            jax.ShapeDtypeStruct((fields, rows, LANES), f32),
            jax.ShapeDtypeStruct((2, fields, levels, LANES), f32),
        ),
        in_specs=[spec(HBM)],
        out_specs=(spec(HBM), spec(HBM), spec(VMEM), spec(VMEM)),
        scratch_shapes=[
            pltpu.VMEM((fields, levels, rows, LANES), f32),
            pltpu.VMEM((fields, levels, rows, LANES), f32),
            pltpu.VMEM((2, fields, levels, LANES), f32),
            pltpu.VMEM((2, fields, levels, LANES), f32),
            pltpu.SemaphoreType.DMA((2, 2 * fields)),
            pltpu.SemaphoreType.DMA((2 + 4 * fields,)),
        ],
        compiler_params=pltpu.CompilerParams(vmem_limit_bytes=VMEM_BYTES),
        cost_estimate=cost(0, 4 * 2 * 4 * fields * levels * width),
    )(ocean_state)


def ice_kernel(
    count,
    listed,
    state,
    strength,
    mass,
    fraction,
    wind,
    surface,
    ice_out,
    stress_out,
    covered,
    su,
    sv,
    sx,
    sy,
    sxy,
    cp,
    cq,
    ca,
    cb,
    gx,
    gy,
):
    rows, width = mass.shape
    blocks = width // BX
    groups = blocks // HALF
    area = rows * HALF

    for s in range(blocks):
        covered[listed[0, s]] = jnp.where(s < count[0], 1, 0)

    def place(block):
        return pl.ds((block // HALF) * area + block % HALF, rows, stride=HALF)

    for b in range(blocks):
        at = slice(b * BX, (b + 1) * BX)
        to = place(b)
        m = mass[:, at]
        inverse = 1.0 / (m + SUB_STEP)
        push = SUB_STEP * inverse
        p = RELAX * strength[:, at]
        su[to, :] = state[0, :, at]
        sv[to, :] = state[1, :, at]
        sx[to, :] = state[2, :, at] + p
        sy[to, :] = state[3, :, at] + p
        sxy[to, :] = state[4, :, at]
        cp[to, :] = p
        cq[to, :] = p * (0.625 * DECAY / 1.25**0.5)
        ca[to, :] = m * inverse
        cb[to, :] = push
        gx[to, :] = wind[0, :, at] + surface[0, 0, :, at]
        gy[to, :] = wind[1, :, at] + surface[1, 0, :, at]

    lane = lane_index(HALF)
    final = lane == LANES - 1
    initial = lane == 0

    def ahead(q):
        return jnp.where(final, 0.0, pltpu.roll(q, LANES - 1, axis=1) - q)

    def behind(q):
        return q - jnp.where(initial, 0.0, pltpu.roll(q, 1, axis=1))

    def vec(g, y):
        return pl.ds(g * area + y * HALF, HALF)

    for g in range(groups):
        for y in range(rows):
            i = vec(g, y)
            p = cp[i, :]
            down = p if y == 0 else p - cp[vec(g, y - 1), :]
            gx[i, :] = cb[i, :] * (gx[i, :] - behind(p))
            gy[i, :] = cb[i, :] * (gy[i, :] - down)

    def sweep(step, carry):
        for _ in range(UNROLL):
            now = [(su[vec(g, 0), :], sv[vec(g, 0), :]) for g in range(groups)]
            above = [None] * groups
            for y in range(rows):
                for g in range(groups):
                    i = vec(g, y)
                    u, v = now[g]
                    ux = ahead(u)
                    shear = ahead(v)
                    if y < rows - 1:
                        j = vec(g, y + 1)
                        un, vn = su[j, :], sv[j, :]
                        now[g] = (un, vn)
                        vy = vn - v
                        shear = shear + (un - u)
                        a = ux + 0.6 * vy
                        b = 0.6 * ux + vy
                        d = ux * a + vy * b
                    else:
                        a = ux
                        b = 0.6 * ux
                        d = ux * a
                    small = 0.2 * shear
                    q = cq[i, :] * lax.rsqrt(d + (shear * small + 0.2))
                    xx = DECAY * sx[i, :] + q * a
                    yy = DECAY * sy[i, :] + q * b
                    xy = DECAY * sxy[i, :] + q * small
                    sx[i, :] = xx
                    sy[i, :] = yy
                    sxy[i, :] = xy
                    fx = behind(xx)
                    fy = behind(xy)
                    if y:
                        fx = fx + (xy - above[g][0])
                        fy = fy + (yy - above[g][1])
                    else:
                        fx = fx + xy
                        fy = fy + yy
                    above[g] = (xy, yy)
                    a0 = ca[i, :]
                    b0 = cb[i, :]
                    su[i, :] = a0 * (u + TURNING * SUB_STEP * v) + (b0 * fx + gx[i, :])
                    sv[i, :] = a0 * (v - TURNING * SUB_STEP * u) + (b0 * fy + gy[i, :])
        return carry

    lax.fori_loop(0, SUBCYCLES // UNROLL, sweep, 0)

    for b in range(blocks):
        at = slice(b * BX, (b + 1) * BX)
        fr = place(b)
        keep = covered[b] == 1
        u = su[fr, :]
        v = sv[fr, :]
        p = cp[fr, :]
        ice_out[0, :, at] = jnp.where(keep, u, state[0, :, at])
        ice_out[1, :, at] = jnp.where(keep, v, state[1, :, at])
        ice_out[2, :, at] = jnp.where(keep, sx[fr, :] - p, state[2, :, at])
        ice_out[3, :, at] = jnp.where(keep, sy[fr, :] - p, state[3, :, at])
        ice_out[4, :, at] = jnp.where(keep, sxy[fr, :], state[4, :, at])
        part = fraction[:, at]
        for d, vel in enumerate((u, v)):
            w = wind[d, :, at]
            merged = part * (vel - surface[d, 0, :, at]) + (1.0 - part) * w
            stress_out[d, :, at] = jnp.where(keep, merged, w)


def ice(ice_state, strength, ice_mass, ice_fraction, wind_stress, ice_count, ice_list, surface):
    rows, width = ice_mass.shape
    f32 = jnp.float32
    cells = (rows * width // BX, BX)
    return pl.pallas_call(
        ice_kernel,
        name="ice_subcycles",
        out_shape=(
            jax.ShapeDtypeStruct(ice_state.shape, f32),
            jax.ShapeDtypeStruct(wind_stress.shape, f32),
        ),
        in_specs=[spec(SMEM)] * 2 + [spec(VMEM)] * 6,
        out_specs=(spec(VMEM), spec(VMEM)),
        scratch_shapes=[pltpu.SMEM((width // BX,), jnp.int32)]
        + [pltpu.VMEM(cells, f32)] * 11,
        compiler_params=pltpu.CompilerParams(vmem_limit_bytes=VMEM_BYTES),
        cost_estimate=cost(SUBCYCLES * 50 * rows * width, 4 * 22 * rows * width),
    )(ice_count, ice_list, ice_state, strength, ice_mass, ice_fraction, wind_stress, surface)


def main_kernel(x_hbm, cols, bih, prev, cor, out_hbm, x, out, in_sem, out_sem):
    fields, levels, rows, width = x.shape
    tiles = width // LANES

    def fetch(k):
        return pltpu.make_async_copy(x_hbm.at[:, k], x.at[:, k], in_sem.at[k])

    def store(k):
        return pltpu.make_async_copy(out.at[:, k], out_hbm.at[:, k], out_sem.at[k])

    for k in range(levels):
        fetch(k).start()

    row = lax.broadcasted_iota(jnp.int32, (HALF, LANES), 0)
    lane = lane_index(HALF)
    top, bottom = row == 0, row == HALF - 1
    initial, final = lane == 0, lane == LANES - 1

    def down(pair):
        ra, rb = (pltpu.roll(h, 1, axis=0) for h in pair)
        return (jnp.where(top, 0.0, ra), jnp.where(top, ra, rb))

    def up(pair):
        ra, rb = (pltpu.roll(h, HALF - 1, axis=0) for h in pair)
        return (jnp.where(bottom, rb, ra), jnp.where(bottom, 0.0, rb))

    def rolled(pair):
        return tuple(
            (pltpu.roll(h, 1, axis=1), pltpu.roll(h, LANES - 1, axis=1)) for h in pair
        )

    def horizontal(west, here, east, centre):
        return tuple(
            jnp.where(initial, west[h][0], here[h][0])
            + jnp.where(final, east[h][1], here[h][1])
            - 4.0 * centre[h]
            for h in range(2)
        )

    def both(ref, *lead, at):
        return (ref[(*lead, slice(0, HALF), at)], ref[(*lead, slice(HALF, rows), at)])

    fetch(0).wait()

    def level(k, carry):
        @pl.when(k + 1 < levels)
        def _():
            fetch(k + 1).wait()

        before = jnp.maximum(k - 1, 0)
        after = jnp.minimum(k + 1, levels - 1)
        shift = lax.rem(LANES - 4 * k, LANES)
        for f in range(fields):
            edge_all = pltpu.roll(cols[f], shift, axis=1)
            edge = (edge_all[0:HALF], edge_all[HALF:rows])

            def load(c):
                if c < 0 or c >= tiles:
                    return edge
                return both(x, f, k, at=slice(c * LANES, (c + 1) * LANES))

            raw = {-1: edge, 0: load(0)}
            turned = {c: rolled(raw[c]) for c in (-1, 0)}
            lastt = load(tiles - 1)
            last_turned = rolled(lastt)
            first_pass = {-1: horizontal(last_turned, turned[-1], turned[0], raw[-1])}
            first_turned = {-1: rolled(first_pass[-1])}

            def advance(c):
                if c + 1 == tiles:
                    raw[c + 1], turned[c + 1] = raw[-1], turned[-1]
                elif c + 1 == tiles - 1:
                    raw[c + 1], turned[c + 1] = lastt, last_turned
                else:
                    raw[c + 1] = load(c + 1)
                    turned[c + 1] = rolled(raw[c + 1])
                if c == tiles:
                    return
                first_pass[c] = horizontal(turned[c - 1], turned[c], turned[c + 1], raw[c])
                first_turned[c] = rolled(first_pass[c])

            advance(0)
            for c in range(tiles):
                if c + 1 < tiles:
                    advance(c + 1)
                else:
                    first_turned[tiles] = first_turned[-1]
                at = slice(c * LANES, (c + 1) * LANES)
                q = raw[c]
                g = first_pass[c]
                second = horizontal(
                    first_turned[c - 1], first_turned[c], first_turned[c + 1], g
                )
                qd, qu = down(q), up(q)
                w = tuple((g[h] + g[h]) + (qd[h] + qu[h]) for h in range(2))
                wd, wu = down(w), up(w)
                coef = both(bih, at=at)
                qb = both(x, f, before, at=at)
                qa = both(x, f, after, at=at)
                for h in range(2):
                    edge_row = top if h == 0 else bottom
                    lap = second[h] + (wd[h] + wu[h]) + jnp.where(edge_row, q[h], 0.0)
                    res = (
                        (1.0 - 2.0 * KV_MIX) * q[h]
                        + KV_MIX * (qb[h] + qa[h])
                        - coef[h] * lap
                    )
                    rs = slice(h * HALF, (h + 1) * HALF)
                    if f == 0:
                        res = res + cor[rs, :] * x[1, k, rs, at]
                    elif f == 1:
                        res = res - cor[rs, :] * x[0, k, rs, at]
                    out[f, k, rs, at] = res

        @pl.when(k == 0)
        def _():
            for d in range(2):
                out[d, 0] = out[d, 0] + prev[d]

        store(k).start()
        return carry

    lax.fori_loop(0, levels, level, 0)
    for k in range(levels):
        store(k).wait()


def ocean(ocean_state, cols, biharmonic, prev_stress, coriolis):
    fields, levels, rows, width = ocean_state.shape
    f32 = jnp.float32
    return pl.pallas_call(
        main_kernel,
        name="ocean_tile",
        out_shape=jax.ShapeDtypeStruct(ocean_state.shape, f32),
        in_specs=[spec(HBM)] + [spec(VMEM)] * 4,
        out_specs=spec(HBM),
        scratch_shapes=[
            pltpu.VMEM(ocean_state.shape, f32),
            pltpu.VMEM(ocean_state.shape, f32),
            pltpu.SemaphoreType.DMA((levels,)),
            pltpu.SemaphoreType.DMA((levels,)),
        ],
        compiler_params=pltpu.CompilerParams(vmem_limit_bytes=VMEM_BYTES),
        cost_estimate=cost(30 * ocean_state.size, 8 * ocean_state.size),
    )(ocean_state, cols, biharmonic, prev_stress, coriolis)


def fix_kernel(base, above, below, cabove, cbelow, bih, out, ha, hb, oa, ob, in_sem, out_sem):
    fields, _, levels, width = ha.shape
    rows = base.shape[2]
    tiles = width // LANES
    fetches, stores = [], []
    for f in range(fields):
        mine, back = [], []
        for j in range(2):
            for side, (buf, first) in enumerate(((oa, 0), (ob, rows - 2))):
                n = (f * 2 + j) * 2 + side
                mine.append(
                    pltpu.make_async_copy(base.at[f, :, first + j, :], buf.at[f, j], in_sem.at[n])
                )
                back.append(
                    pltpu.make_async_copy(buf.at[f, j], out.at[f, :, first + j, :], out_sem.at[n])
                )
        n = 4 * fields + 2 * f
        mine.append(pltpu.make_async_copy(above.at[f], ha.at[f], in_sem.at[n]))
        mine.append(pltpu.make_async_copy(below.at[f], hb.at[f], in_sem.at[n + 1]))
        fetches.append(mine)
        stores.append(back)
        for copy in mine:
            copy.start()

    lane = lane_index(HALF)
    initial, final = lane == 0, lane == LANES - 1

    for f in range(fields):
        for copy in fetches[f]:
            copy.wait()
        for halo, corner, near, far, buf, n1, n2 in (
            (ha, cabove, 1, 0, oa, 0, 1),
            (hb, cbelow, 0, 1, ob, 1, 0),
        ):
            r1 = n1 if buf is oa else rows - 2 + n1
            r2 = n2 if buf is oa else rows - 2 + n2

            def octet(s, carry):
                ks = pl.ds(pl.multiple_of(s * HALF, HALF), HALF)
                ext = corner[f, ks, :]
                ext_e, ext_w = pltpu.roll(ext, 1, axis=1), pltpu.roll(ext, LANES - 1, axis=1)
                cur = halo[f, near, ks, 0:LANES]
                west = ext_e
                cur_e, cur_w = pltpu.roll(cur, 1, axis=1), pltpu.roll(cur, LANES - 1, axis=1)
                for c in range(tiles):
                    at = slice(c * LANES, (c + 1) * LANES)
                    if c + 1 < tiles:
                        nxt = halo[f, near, ks, (c + 1) * LANES : (c + 2) * LANES]
                        nxt_e = pltpu.roll(nxt, 1, axis=1)
                        nxt_w = pltpu.roll(nxt, LANES - 1, axis=1)
                    else:
                        nxt, nxt_e, nxt_w = ext, ext_e, ext_w
                    around = jnp.where(initial, west, cur_e) + jnp.where(final, nxt_w, cur_w)
                    lap = halo[f, far, ks, at] + 2.0 * around - 8.0 * cur
                    buf[f, n1, ks, at] = buf[f, n1, ks, at] - bih[r1 : r1 + 1, at] * lap
                    buf[f, n2, ks, at] = buf[f, n2, ks, at] - bih[r2 : r2 + 1, at] * cur
                    west = cur_e
                    cur, cur_e, cur_w = nxt, nxt_e, nxt_w
                return carry

            lax.fori_loop(0, levels // HALF, octet, 0)
        for copy in stores[f]:
            copy.start()
    for back in stores:
        for copy in back:
            copy.wait()


def fix(base, above, below, cabove, cbelow, biharmonic):
    fields, levels, rows, width = base.shape
    f32 = jnp.float32
    edge = pltpu.VMEM((fields, 2, levels, width), f32)
    return pl.pallas_call(
        fix_kernel,
        name="ocean_edges",
        out_shape=jax.ShapeDtypeStruct(base.shape, f32),
        in_specs=[spec(HBM)] * 3 + [spec(VMEM)] * 3,
        out_specs=spec(HBM),
        input_output_aliases={0: 0},
        scratch_shapes=[
            edge,
            edge,
            edge,
            edge,
            pltpu.SemaphoreType.DMA((6 * fields,)),
            pltpu.SemaphoreType.DMA((4 * fields,)),
        ],
        compiler_params=pltpu.CompilerParams(vmem_limit_bytes=VMEM_BYTES),
        cost_estimate=cost(0, 3 * 4 * 4 * fields * levels * width),
    )(base, above, below, cabove, cbelow, biharmonic)


def per_device(
    ocean_state,
    biharmonic,
    prev_stress,
    ice_state,
    strength,
    ice_mass,
    ice_fraction,
    wind_stress,
    ice_count,
    ice_list,
):
    tile_rows = ocean_state.shape[2]
    n_tile = lax.axis_size("tile")
    n_grp = lax.axis_size("grp")

    first, last, cols, corners = pack(ocean_state)

    def shift(value, tile_step, grp_step):
        pairs = []
        for g in range(n_grp):
            for t in range(n_tile):
                if 0 <= t + tile_step < n_tile:
                    target = (g + grp_step) % n_grp
                    pairs.append((g * n_tile + t, target * n_tile + t + tile_step))
        return lax.ppermute(value, ("grp", "tile"), pairs)

    lane = jnp.arange(LANES)

    def around(value, tile_step, eastern):
        west = shift(value, tile_step, 1)
        if n_grp == 2:
            return west
        return jnp.where(eastern, shift(value, tile_step, -1), west)

    above = shift(last, 1, 0)
    below = shift(first, -1, 0)
    cols = around(cols, 0, lane % 4 < 2)
    cabove = around(corners[1], 1, lane < LANES // 2)
    cbelow = around(corners[0], -1, lane < LANES // 2)

    ice_in = (ice_state, strength, ice_mass, ice_fraction, wind_stress, ice_count, ice_list)
    surface = ocean_state[0:2, 0:1]
    ice_out, stress_out = ice(*ice_in, surface)

    rows = (lax.axis_index("tile") * tile_rows + jnp.arange(tile_rows)).astype(jnp.float32) + 0.5
    coriolis = CORIOLIS * (2.0 * rows / (tile_rows * n_tile) - 1.0)
    coriolis = jnp.broadcast_to(coriolis[:, None], (tile_rows, LANES))
    base = ocean(ocean_state, cols, biharmonic, prev_stress, coriolis)
    ocean_out = fix(base, above, below, cabove, cbelow, biharmonic)
    return (ocean_out, ice_out, stress_out)


def solution(mesh):
    placed = (
        P(None, None, "tile", "grp"),
        P("tile", "grp"),
        P(None, "tile", "grp"),
        P(None, "tile", "grp"),
        P("tile", "grp"),
        P("tile", "grp"),
        P("tile", "grp"),
        P(None, "tile", "grp"),
        P(("grp", "tile")),
        P(("grp", "tile"), None),
    )
    return jax.shard_map(
        per_device,
        mesh=mesh,
        in_specs=placed,
        out_specs=(P(None, None, "tile", "grp"), P(None, "tile", "grp"), P(None, "tile", "grp")),
        check_vma=False,
    )
```

```python
import jax
import jax.numpy as jnp
import numpy as np
from jax import lax
from jax.experimental import pallas as pl
from jax.experimental.pallas import tpu as pltpu
from jax.sharding import PartitionSpec as P

BY = 16
BX = 128
SUBCYCLES = 64
UNROLL = 4
LANES = 128
HALF = 8

KV_MIX = 0.2
RELAX = 0.5
SUB_STEP = 0.3
TURNING = 0.3
CORIOLIS = 0.2

DECAY = 1.0 / (1.0 + RELAX)
VMEM_BYTES = 48 * 1024 * 1024

HBM = pltpu.HBM
VMEM = pltpu.VMEM
SMEM = pltpu.SMEM


def spec(space):
    return pl.BlockSpec(memory_space=space)


def cost(flops, nbytes):
    return pl.CostEstimate(flops=flops, bytes_accessed=nbytes, transcendentals=0)


def lane_index(rows):
    return lax.broadcasted_iota(jnp.int32, (rows, LANES), 1)


def pack_kernel(x, first, last, cols, ctop, cbottom, left, right, row_sem, col_sem):
    rows, width = x.shape[2:]
    copies = []
    for j in range(2):
        for side, (to, row) in enumerate(((first, j), (last, rows - 2 + j))):
            copies.append(
                pltpu.make_async_copy(x.at[:, :, row, :], to.at[:, j], row_sem.at[side, j])
            )
    col_copies = []
    for r in range(rows):
        for side, (to, start) in enumerate(((left, 0), (right, width - LANES))):
            col_copies.append(
                pltpu.make_async_copy(
                    x.at[:, :, r, start : start + LANES], to.at[:, r], col_sem.at[side, r]
                )
            )
    for copy in copies + col_copies:
        copy.start()
    for copy in col_copies:
        copy.wait()
    lane = lax.broadcasted_iota(jnp.int32, left.shape[2:], 1)
    for f in range(left.shape[0]):
        for r in range(rows):
            edge = jnp.where(lane < LANES // 2, left[f, r], right[f, r])
            cols[f, r] = edge
            if r == 0:
                ctop[f] = edge
            if r == rows - 1:
                cbottom[f] = edge
    for copy in copies:
        copy.wait()


def pack(ocean_state):
    fields, levels, rows, width = ocean_state.shape
    f32 = jnp.float32
    edge = (fields, rows, levels, LANES)
    return pl.pallas_call(
        pack_kernel,
        name="pack_edges",
        out_shape=(
            jax.ShapeDtypeStruct((fields, 2, levels, width), f32),
            jax.ShapeDtypeStruct((fields, 2, levels, width), f32),
            jax.ShapeDtypeStruct(edge, f32),
            jax.ShapeDtypeStruct((fields, levels, LANES), f32),
            jax.ShapeDtypeStruct((fields, levels, LANES), f32),
        ),
        in_specs=[spec(HBM)],
        out_specs=(spec(VMEM),) * 5,
        scratch_shapes=[
            pltpu.VMEM(edge, f32),
            pltpu.VMEM(edge, f32),
            pltpu.SemaphoreType.DMA((2, 2)),
            pltpu.SemaphoreType.DMA((2, rows)),
        ],
        compiler_params=pltpu.CompilerParams(vmem_limit_bytes=VMEM_BYTES),
        cost_estimate=cost(0, 4 * 2 * 4 * fields * levels * width),
    )(ocean_state)


def split(q, parts):
    out = []
    for _ in range(parts):
        part = q.astype(jnp.bfloat16)
        out.append(part)
        q = q - part.astype(jnp.float32)
    return out


def reorder(value, matrix):
    total = None
    for part in split(value, 3):
        term = jnp.dot(part, matrix, preferred_element_type=jnp.float32)
        total = term if total is None else total + term
    return total


def ice_kernel(
    count,
    listed,
    state,
    strength,
    mass,
    fraction,
    wind,
    surface,
    forward,
    backward,
    ice_out,
    stress_out,
    covered,
    su,
    sv,
    sx,
    sy,
    sxy,
    cp,
    cq,
    ca,
    cb,
    gx,
    gy,
):
    rows, width = mass.shape
    wide = 2 * BX
    pairs = width // wide
    area = rows * pairs
    blocks = width // BX

    for s in range(blocks):
        covered[listed[0, s]] = jnp.where(s < count[0], 1, 0)

    def chunk(j):
        return slice(j * wide, (j + 1) * wide)

    def place(j, odd):
        return pl.ds(odd * area + j, rows, stride=pairs)

    def enter(ref, get):
        value = jnp.concatenate([get(chunk(j)) for j in range(pairs)], axis=0)
        value = reorder(value, forward[...])
        for j in range(pairs):
            for odd in range(2):
                ref[place(j, odd), :] = value[
                    j * rows : (j + 1) * rows, odd * BX : (odd + 1) * BX
                ]

    def leave(ref):
        value = jnp.concatenate(
            [
                jnp.concatenate([ref[place(j, 0), :], ref[place(j, 1), :]], axis=1)
                for j in range(pairs)
            ],
            axis=0,
        )
        return reorder(value, backward[...])

    enter(su, lambda at: state[0, :, at])
    enter(sv, lambda at: state[1, :, at])
    enter(sx, lambda at: state[2, :, at])
    enter(sy, lambda at: state[3, :, at])
    enter(sxy, lambda at: state[4, :, at])
    enter(cp, lambda at: strength[:, at])
    enter(ca, lambda at: mass[:, at])
    enter(gx, lambda at: wind[0, :, at] + surface[0, 0, :, at])
    enter(gy, lambda at: wind[1, :, at] + surface[1, 0, :, at])

    lane = lane_index(pairs)
    final = (lane & (BX // 2 - 1)) == BX // 2 - 1
    initial = (lane & (BX // 2 - 1)) == 0

    def ahead(even, odd):
        return (
            odd - even,
            jnp.where(final, 0.0, pltpu.roll(even, LANES - 1, axis=1) - odd),
        )

    def behind(even, odd):
        return (
            even - jnp.where(initial, 0.0, pltpu.roll(odd, 1, axis=1)),
            odd - even,
        )

    def vec(odd, y):
        return pl.ds(odd * area + y * pairs, pairs)

    def row_of(ref, y):
        return (ref[vec(0, y), :], ref[vec(1, y), :])

    below = None
    for y in range(rows):
        p = tuple(RELAX * s for s in row_of(cp, y))
        across = behind(*p)
        for odd in range(2):
            i = vec(odd, y)
            m = ca[i, :]
            inverse = 1.0 / (m + SUB_STEP)
            push = SUB_STEP * inverse
            down = p[odd] if y == 0 else p[odd] - below[odd]
            gx[i, :] = push * (gx[i, :] - across[odd])
            gy[i, :] = push * (gy[i, :] - down)
            ca[i, :] = m * inverse
            cb[i, :] = push
            cq[i, :] = p[odd] * (0.625 * DECAY / 1.25**0.5)
            cp[i, :] = p[odd]
            sx[i, :] = sx[i, :] + p[odd]
            sy[i, :] = sy[i, :] + p[odd]
        below = p

    def sweep(step, carry):
        for _ in range(UNROLL):
            u, v = row_of(su, 0), row_of(sv, 0)
            above = None
            for y in range(rows):
                ux, vx = ahead(*u), ahead(*v)
                xx, yy, xy = [], [], []
                if y < rows - 1:
                    un, vn = row_of(su, y + 1), row_of(sv, y + 1)
                for odd in range(2):
                    i = vec(odd, y)
                    shear = vx[odd]
                    if y < rows - 1:
                        vy = vn[odd] - v[odd]
                        shear = shear + (un[odd] - u[odd])
                        a = ux[odd] + 0.6 * vy
                        b = 0.6 * ux[odd] + vy
                        d = ux[odd] * a + vy * b
                    else:
                        a = ux[odd]
                        b = 0.6 * a
                        d = a * a
                    small = 0.2 * shear
                    q = cq[i, :] * lax.rsqrt(d + (shear * small + 0.2))
                    xx.append(DECAY * sx[i, :] + q * a)
                    yy.append(DECAY * sy[i, :] + q * b)
                    xy.append(DECAY * sxy[i, :] + q * small)
                fx, fy = behind(*xx), behind(*xy)
                for odd in range(2):
                    i = vec(odd, y)
                    sx[i, :] = xx[odd]
                    sy[i, :] = yy[odd]
                    sxy[i, :] = xy[odd]
                    if y:
                        fxo = fx[odd] + (xy[odd] - above[0][odd])
                        fyo = fy[odd] + (yy[odd] - above[1][odd])
                    else:
                        fxo = fx[odd] + xy[odd]
                        fyo = fy[odd] + yy[odd]
                    a0 = ca[i, :]
                    b0 = cb[i, :]
                    uo, vo = u[odd], v[odd]
                    su[i, :] = a0 * (uo + TURNING * SUB_STEP * vo) + (b0 * fxo + gx[i, :])
                    sv[i, :] = a0 * (vo - TURNING * SUB_STEP * uo) + (b0 * fyo + gy[i, :])
                above = (xy, yy)
                if y < rows - 1:
                    u, v = un, vn
        return carry

    lax.fori_loop(0, SUBCYCLES // UNROLL, sweep, 0)

    sx[...] = sx[...] - cp[...]
    sy[...] = sy[...] - cp[...]
    for n, ref in enumerate((su, sv, sx, sy, sxy)):
        value = leave(ref)
        for b in range(blocks):
            at = slice(b * BX, (b + 1) * BX)
            new = value[(b // 2) * rows : (b // 2 + 1) * rows, (b % 2) * BX : (b % 2 + 1) * BX]
            keep = covered[b] == 1
            ice_out[n, :, at] = jnp.where(keep, new, state[n, :, at])
            if n < 2:
                part = fraction[:, at]
                w = wind[n, :, at]
                merged = part * (new - surface[n, 0, :, at]) + (1.0 - part) * w
                stress_out[n, :, at] = jnp.where(keep, merged, w)


def ice(ice_state, strength, ice_mass, ice_fraction, wind_stress, ice_count, ice_list, surface):
    rows, width = ice_mass.shape
    f32 = jnp.float32
    cells = (rows * width // BX, BX)
    wide = 2 * BX
    lanes = np.arange(wide)
    target = (lanes % 2) * BX + (lanes // BX) * (BX // 2) + (lanes % BX) // 2
    matrix = np.zeros((wide, wide), np.float32)
    matrix[lanes, target] = 1.0
    forward = jnp.asarray(matrix, jnp.bfloat16)
    backward = jnp.asarray(matrix.T, jnp.bfloat16)
    return pl.pallas_call(
        ice_kernel,
        name="ice_subcycles",
        out_shape=(
            jax.ShapeDtypeStruct(ice_state.shape, f32),
            jax.ShapeDtypeStruct(wind_stress.shape, f32),
        ),
        in_specs=[spec(SMEM)] * 2 + [spec(VMEM)] * 8,
        out_specs=(spec(VMEM), spec(VMEM)),
        scratch_shapes=[pltpu.SMEM((width // BX,), jnp.int32)]
        + [pltpu.VMEM(cells, f32)] * 11,
        compiler_params=pltpu.CompilerParams(vmem_limit_bytes=VMEM_BYTES),
        cost_estimate=cost(SUBCYCLES * 50 * rows * width, 4 * 22 * rows * width),
    )(
        ice_count,
        ice_list,
        ice_state,
        strength,
        ice_mass,
        ice_fraction,
        wind_stress,
        surface,
        forward,
        backward,
    )


WIDE = 256
FETCH = 512


def column_matrix():
    double = {0: 20.0, 1: -8.0, 2: 1.0}
    single = {0: -8.0, 1: 2.0}
    own = np.zeros((WIDE, 2 * WIDE), np.float32)
    side = np.zeros((LANES, 2 * WIDE), np.float32)
    for j in range(WIDE):
        for n, taps in enumerate((double, single)):
            for d, value in taps.items():
                for i in {j - d, j + d}:
                    if 0 <= i < WIDE:
                        own[i, n * WIDE + j] = value
                    else:
                        side[i % LANES, n * WIDE + j] = value
    return np.concatenate([own, own, side, side], axis=0)


def main_kernel(x_hbm, cols, bih, prev, cor, matrix, out_hbm, x, out, y, in_sem, out_sem):
    fields, rows, levels, width = x.shape
    steps = width // WIDE
    spans = width // FETCH
    each = FETCH // WIDE

    def fetches(s):
        at = slice(s * FETCH, (s + 1) * FETCH)
        return [
            pltpu.make_async_copy(x_hbm.at[:, :, r, at], x.at[:, r, :, at], in_sem.at[s, r])
            for r in range(rows)
        ]

    def stores(s):
        at = slice(s * FETCH, (s + 1) * FETCH)
        return [
            pltpu.make_async_copy(out.at[:, r, :, at], out_hbm.at[:, :, r, at], out_sem.at[s, r])
            for r in range(rows)
        ]

    for s in range(spans):
        for copy in fetches(s):
            copy.start()

    level = lax.broadcasted_iota(jnp.int32, (levels, WIDE), 0)
    lane = lax.broadcasted_iota(jnp.int32, (rows * levels, LANES), 1)
    surface, deepest = level == 0, level == levels - 1

    def merge(value):
        return value.reshape(rows * levels, value.shape[-1])

    waited = 0
    for m in range(steps):
        need = min((m + 1) // each, spans - 1)
        while waited <= need:
            for copy in fetches(waited):
                copy.wait()
            waited += 1
        at = slice(m * WIDE, (m + 1) * WIDE)
        for f in range(fields):
            slot = (m * fields + f) % 2
            own = merge(x[f, :, :, at])
            if m == 0:
                west = merge(cols[f])
            else:
                west = merge(x[f, :, :, m * WIDE - LANES : m * WIDE])
            if m == steps - 1:
                east = merge(cols[f])
            else:
                east = merge(x[f, :, :, (m + 1) * WIDE : (m + 1) * WIDE + LANES])
            side = jnp.where(lane < LANES // 2, east, west)
            y[slot] = jnp.dot(
                jnp.concatenate(split(own, 2) + split(side, 2), axis=1),
                matrix[...],
                preferred_element_type=jnp.float32,
            )

            def near(r):
                return y[slot, r * levels : (r + 1) * levels, WIDE : 2 * WIDE]

            for r in range(rows):
                q = x[f, r, :, at]
                lap = y[slot, r * levels : (r + 1) * levels, 0:WIDE]
                for step in (-1, 1):
                    if 0 <= r + step < rows:
                        lap = lap + near(r + step)
                    if 0 <= r + 2 * step < rows:
                        lap = lap + x[f, r + 2 * step, :, at]
                qb = jnp.where(surface, q, pltpu.roll(q, 1, axis=0))
                qa = jnp.where(deepest, q, pltpu.roll(q, levels - 1, axis=0))
                res = (1.0 - 2.0 * KV_MIX) * q + KV_MIX * (qb + qa) - bih[r : r + 1, at] * lap
                if f == 0:
                    res = res + cor[r] * x[1, r, :, at]
                elif f == 1:
                    res = res - cor[r] * x[0, r, :, at]
                if f < 2:
                    res = res + jnp.where(surface, prev[f, r : r + 1, at], 0.0)
                out[f, r, :, at] = res
        if m % each == each - 1:
            for copy in stores(m // each):
                copy.start()
    for s in range(spans):
        for copy in stores(s):
            copy.wait()


def ocean(ocean_state, cols, biharmonic, prev_stress, coriolis):
    fields, levels, rows, width = ocean_state.shape
    f32 = jnp.float32
    matrix = jnp.asarray(column_matrix(), jnp.bfloat16)
    held = (fields, rows, levels, width)
    return pl.pallas_call(
        main_kernel,
        name="ocean_tile",
        out_shape=jax.ShapeDtypeStruct(ocean_state.shape, f32),
        in_specs=[spec(HBM)] + [spec(VMEM)] * 3 + [spec(SMEM), spec(VMEM)],
        out_specs=spec(HBM),
        scratch_shapes=[
            pltpu.VMEM(held, f32),
            pltpu.VMEM(held, f32),
            pltpu.VMEM((2, rows * levels, 2 * WIDE), f32),
            pltpu.SemaphoreType.DMA((width // FETCH, rows)),
            pltpu.SemaphoreType.DMA((width // FETCH, rows)),
        ],
        compiler_params=pltpu.CompilerParams(vmem_limit_bytes=VMEM_BYTES),
        cost_estimate=cost(30 * ocean_state.size, 8 * ocean_state.size),
    )(ocean_state, cols, biharmonic, prev_stress, coriolis, matrix)


def fix_kernel(base, above, below, cabove, cbelow, bih, out, ha, hb, oa, ob, in_sem, out_sem):
    fields, _, levels, width = ha.shape
    rows = base.shape[2]
    tiles = width // LANES
    fetches, stores = [], []
    for f in range(fields):
        mine, back = [], []
        for j in range(2):
            for side, (buf, first) in enumerate(((oa, 0), (ob, rows - 2))):
                n = (f * 2 + j) * 2 + side
                mine.append(
                    pltpu.make_async_copy(base.at[f, :, first + j, :], buf.at[f, j], in_sem.at[n])
                )
                back.append(
                    pltpu.make_async_copy(buf.at[f, j], out.at[f, :, first + j, :], out_sem.at[n])
                )
        n = 4 * fields + 2 * f
        mine.append(pltpu.make_async_copy(above.at[f], ha.at[f], in_sem.at[n]))
        mine.append(pltpu.make_async_copy(below.at[f], hb.at[f], in_sem.at[n + 1]))
        fetches.append(mine)
        stores.append(back)
        for copy in mine:
            copy.start()

    lane = lane_index(HALF)
    initial, final = lane == 0, lane == LANES - 1

    for f in range(fields):
        for copy in fetches[f]:
            copy.wait()
        for halo, corner, near, far, buf, n1, n2 in (
            (ha, cabove, 1, 0, oa, 0, 1),
            (hb, cbelow, 0, 1, ob, 1, 0),
        ):
            r1 = n1 if buf is oa else rows - 2 + n1
            r2 = n2 if buf is oa else rows - 2 + n2

            def octet(s, carry):
                ks = pl.ds(pl.multiple_of(s * HALF, HALF), HALF)
                ext = corner[f, ks, :]
                ext_e, ext_w = pltpu.roll(ext, 1, axis=1), pltpu.roll(ext, LANES - 1, axis=1)
                cur = halo[f, near, ks, 0:LANES]
                west = ext_e
                cur_e, cur_w = pltpu.roll(cur, 1, axis=1), pltpu.roll(cur, LANES - 1, axis=1)
                for c in range(tiles):
                    at = slice(c * LANES, (c + 1) * LANES)
                    if c + 1 < tiles:
                        nxt = halo[f, near, ks, (c + 1) * LANES : (c + 2) * LANES]
                        nxt_e = pltpu.roll(nxt, 1, axis=1)
                        nxt_w = pltpu.roll(nxt, LANES - 1, axis=1)
                    else:
                        nxt, nxt_e, nxt_w = ext, ext_e, ext_w
                    around = jnp.where(initial, west, cur_e) + jnp.where(final, nxt_w, cur_w)
                    lap = halo[f, far, ks, at] + 2.0 * around - 8.0 * cur
                    buf[f, n1, ks, at] = buf[f, n1, ks, at] - bih[r1 : r1 + 1, at] * lap
                    buf[f, n2, ks, at] = buf[f, n2, ks, at] - bih[r2 : r2 + 1, at] * cur
                    west = cur_e
                    cur, cur_e, cur_w = nxt, nxt_e, nxt_w
                return carry

            lax.fori_loop(0, levels // HALF, octet, 0)
        for copy in stores[f]:
            copy.start()
    for back in stores:
        for copy in back:
            copy.wait()


def fix(base, above, below, cabove, cbelow, biharmonic):
    fields, levels, rows, width = base.shape
    f32 = jnp.float32
    edge = pltpu.VMEM((fields, 2, levels, width), f32)
    return pl.pallas_call(
        fix_kernel,
        name="ocean_edges",
        out_shape=jax.ShapeDtypeStruct(base.shape, f32),
        in_specs=[spec(HBM)] * 3 + [spec(VMEM)] * 3,
        out_specs=spec(HBM),
        input_output_aliases={0: 0},
        scratch_shapes=[
            edge,
            edge,
            edge,
            edge,
            pltpu.SemaphoreType.DMA((6 * fields,)),
            pltpu.SemaphoreType.DMA((4 * fields,)),
        ],
        compiler_params=pltpu.CompilerParams(vmem_limit_bytes=VMEM_BYTES),
        cost_estimate=cost(0, 3 * 4 * 4 * fields * levels * width),
    )(base, above, below, cabove, cbelow, biharmonic)


def per_device(
    ocean_state,
    biharmonic,
    prev_stress,
    ice_state,
    strength,
    ice_mass,
    ice_fraction,
    wind_stress,
    ice_count,
    ice_list,
):
    tile_rows = ocean_state.shape[2]
    n_tile = lax.axis_size("tile")
    n_grp = lax.axis_size("grp")

    first, last, cols, ctop, cbottom = pack(ocean_state)

    def shift(value, tile_step, grp_step):
        pairs = []
        for g in range(n_grp):
            for t in range(n_tile):
                if 0 <= t + tile_step < n_tile:
                    target = (g + grp_step) % n_grp
                    pairs.append((g * n_tile + t, target * n_tile + t + tile_step))
        return lax.ppermute(value, ("grp", "tile"), pairs)

    lane = jnp.arange(LANES)

    def around(value, tile_step, eastern):
        west = shift(value, tile_step, 1)
        if n_grp == 2:
            return west
        return jnp.where(eastern, shift(value, tile_step, -1), west)

    above = shift(last, 1, 0)
    below = shift(first, -1, 0)
    cols = around(cols, 0, lane < LANES // 2)
    cabove = around(cbottom, 1, lane < LANES // 2)
    cbelow = around(ctop, -1, lane < LANES // 2)

    ice_in = (ice_state, strength, ice_mass, ice_fraction, wind_stress, ice_count, ice_list)
    surface = ocean_state[0:2, 0:1]
    ice_out, stress_out = ice(*ice_in, surface)

    rows = (lax.axis_index("tile") * tile_rows + jnp.arange(tile_rows)).astype(jnp.float32) + 0.5
    coriolis = CORIOLIS * (2.0 * rows / (tile_rows * n_tile) - 1.0)
    base = ocean(ocean_state, cols, biharmonic, prev_stress, coriolis)
    ocean_out = fix(base, above, below, cabove, cbelow, biharmonic)
    return (ocean_out, ice_out, stress_out)


def solution(mesh):
    placed = (
        P(None, None, "tile", "grp"),
        P("tile", "grp"),
        P(None, "tile", "grp"),
        P(None, "tile", "grp"),
        P("tile", "grp"),
        P("tile", "grp"),
        P("tile", "grp"),
        P(None, "tile", "grp"),
        P(("grp", "tile")),
        P(("grp", "tile"), None),
    )
    return jax.shard_map(
        per_device,
        mesh=mesh,
        in_specs=placed,
        out_specs=(P(None, None, "tile", "grp"), P(None, "tile", "grp"), P(None, "tile", "grp")),
        check_vma=False,
    )
```

```python
import jax
import jax.numpy as jnp
from jax import lax
from jax.experimental import pallas as pl
from jax.experimental.pallas import tpu as pltpu
from jax.sharding import PartitionSpec as P

BY = 16
BX = 128
SUBCYCLES = 64
UNROLL = 4
LANES = 128
HALF = 8

KV_MIX = 0.2
RELAX = 0.5
SUB_STEP = 0.3
TURNING = 0.3
CORIOLIS = 0.2

DECAY = 1.0 / (1.0 + RELAX)
VMEM_BYTES = 48 * 1024 * 1024

HBM = pltpu.HBM
VMEM = pltpu.VMEM
SMEM = pltpu.SMEM


def spec(space):
    return pl.BlockSpec(memory_space=space)


def cost(flops, nbytes):
    return pl.CostEstimate(flops=flops, bytes_accessed=nbytes, transcendentals=0)


def lane_index(rows):
    return lax.broadcasted_iota(jnp.int32, (rows, LANES), 1)


WIDE = 256
FETCH = 512
GROUP = 4


def iota(shape, dim):
    return lax.broadcasted_iota(jnp.int32, shape, dim)


def as_matrix(value):
    return value.astype(jnp.float32).astype(jnp.bfloat16)


def column_taps(source, shape):
    place = iota(shape, 1)
    d = jnp.abs(source - (place & (WIDE - 1)))
    double = jnp.where(d == 0, 20, jnp.where(d == 1, -8, jnp.where(d == 2, 1, 0)))
    single = jnp.where(d == 0, -8, jnp.where(d == 1, 2, 0))
    return as_matrix(jnp.where(place < WIDE, double, single))


def make_columns(matrix):
    own = (WIDE, 2 * WIDE)
    taps = column_taps(iota(own, 0), own)
    matrix[0:WIDE, :] = taps
    matrix[WIDE : 2 * WIDE, :] = taps
    side = (LANES, 2 * WIDE)
    lane = iota(side, 0)
    taps = column_taps(jnp.where(lane < LANES // 2, lane + WIDE, lane - LANES), side)
    matrix[2 * WIDE : 2 * WIDE + LANES, :] = taps
    matrix[2 * WIDE + LANES : 2 * WIDE + 2 * LANES, :] = taps


def make_mixing(mixing, levels):
    height = GROUP * levels
    shape = mixing.shape
    a, c = iota(shape, 0), iota(shape, 1)
    c = jnp.where(c >= height, c - height, c)

    def parts(index):
        group = jnp.zeros(shape, jnp.int32)
        for n in range(1, GROUP):
            group = group + jnp.where(index >= n * levels, 1, 0)
        return group, index - levels * group

    ga, la = parts(a)
    gc, lc = parts(c)
    value = (
        jnp.where(lc == jnp.maximum(la - 1, 0), 1, 0)
        + jnp.where(lc == jnp.minimum(la + 1, levels - 1), 1, 0)
        - jnp.where(lc == la, 2, 0)
    )
    mixing[...] = as_matrix(jnp.where(ga == gc, value, 0))


def make_orders(forward, backward):
    shape = forward.shape

    def target(i):
        return ((i & 1) * BX) + ((i >> 7) * (BX // 2)) + ((i & (BX - 1)) >> 1)

    forward[...] = as_matrix(jnp.where(target(iota(shape, 0)) == iota(shape, 1), 1, 0))
    backward[...] = as_matrix(jnp.where(target(iota(shape, 1)) == iota(shape, 0), 1, 0))


def pack_kernel(
    x,
    first,
    last,
    cols,
    matrix,
    mixing,
    forward,
    backward,
    left,
    right,
    row_sem,
    col_sem,
):
    rows, width = x.shape[2:]
    copies = []
    for j in range(2):
        for side, (to, row) in enumerate(((first, j), (last, rows - 2 + j))):
            copies.append(
                pltpu.make_async_copy(x.at[:, :, row, :], to.at[j], row_sem.at[side, j])
            )
    col_copies = []
    for r in range(rows):
        for side, (to, start) in enumerate(((left, 0), (right, width - LANES))):
            col_copies.append(
                pltpu.make_async_copy(
                    x.at[:, :, r, start : start + LANES], to.at[:, r], col_sem.at[side, r]
                )
            )
    for copy in copies + col_copies:
        copy.start()
    make_columns(matrix)
    make_mixing(mixing, x.shape[1])
    make_orders(forward, backward)
    for copy in col_copies:
        copy.wait()
    lane = lax.broadcasted_iota(jnp.int32, left.shape[2:], 1)
    for f in range(left.shape[0]):
        for r in range(rows):
            cols[f, r] = jnp.where(lane < LANES // 2, left[f, r], right[f, r])
    for copy in copies:
        copy.wait()


def pack(ocean_state):
    fields, levels, rows, width = ocean_state.shape
    f32 = jnp.float32
    edge = (fields, rows, levels, LANES)
    return pl.pallas_call(
        pack_kernel,
        name="pack_edges",
        out_shape=(
            jax.ShapeDtypeStruct((2, fields, levels, width), f32),
            jax.ShapeDtypeStruct((2, fields, levels, width), f32),
            jax.ShapeDtypeStruct(edge, f32),
            jax.ShapeDtypeStruct((2 * (WIDE + LANES), 2 * WIDE), jnp.bfloat16),
            jax.ShapeDtypeStruct((GROUP * levels, 2 * GROUP * levels), jnp.bfloat16),
            jax.ShapeDtypeStruct((2 * BX, 2 * BX), jnp.bfloat16),
            jax.ShapeDtypeStruct((2 * BX, 2 * BX), jnp.bfloat16),
        ),
        in_specs=[spec(HBM)],
        out_specs=(spec(VMEM),) * 7,
        scratch_shapes=[
            pltpu.VMEM(edge, f32),
            pltpu.VMEM(edge, f32),
            pltpu.SemaphoreType.DMA((2, 2)),
            pltpu.SemaphoreType.DMA((2, rows)),
        ],
        compiler_params=pltpu.CompilerParams(vmem_limit_bytes=VMEM_BYTES),
        cost_estimate=cost(0, 4 * 2 * 4 * fields * levels * width),
    )(ocean_state)


def split(q, parts):
    out = []
    for _ in range(parts):
        part = q.astype(jnp.bfloat16)
        out.append(part)
        q = q - part.astype(jnp.float32)
    return out


def reorder(value, matrix):
    total = None
    for part in split(value, 3):
        term = jnp.dot(part, matrix, preferred_element_type=jnp.float32)
        total = term if total is None else total + term
    return total


def ice_kernel(
    count,
    listed,
    state_hbm,
    strength_hbm,
    mass_hbm,
    fraction_hbm,
    wind_hbm,
    ocean_hbm,
    forward,
    backward,
    ice_out,
    stress_out,
    state,
    strength,
    mass,
    fraction,
    wind,
    surface,
    sem,
    covered,
    su,
    sv,
    sx,
    sy,
    sxy,
    cp,
    cq,
    ca,
    cb,
    gx,
    gy,
):
    rows, width = mass.shape
    wide = 2 * BX
    pairs = width // wide
    area = rows * pairs
    blocks = width // BX

    copies = [
        pltpu.make_async_copy(source, to, sem.at[n])
        for n, (source, to) in enumerate(
            (
                (state_hbm, state),
                (strength_hbm, strength),
                (mass_hbm, mass),
                (wind_hbm, wind),
                (ocean_hbm.at[0, 0], surface.at[0]),
                (ocean_hbm.at[1, 0], surface.at[1]),
                (fraction_hbm, fraction),
            )
        )
    ]
    for copy in copies:
        copy.start()

    for s in range(blocks):
        covered[listed[0, s]] = jnp.where(s < count[0], 1, 0)

    def chunk(j):
        return slice(j * wide, (j + 1) * wide)

    def place(j, odd):
        return pl.ds(odd * area + j, rows, stride=pairs)

    def enter(ref, get):
        value = jnp.concatenate([get(chunk(j)) for j in range(pairs)], axis=0)
        value = reorder(value, forward[...])
        for j in range(pairs):
            for odd in range(2):
                ref[place(j, odd), :] = value[
                    j * rows : (j + 1) * rows, odd * BX : (odd + 1) * BX
                ]

    def leave(ref):
        value = jnp.concatenate(
            [
                jnp.concatenate([ref[place(j, 0), :], ref[place(j, 1), :]], axis=1)
                for j in range(pairs)
            ],
            axis=0,
        )
        return reorder(value, backward[...])

    copies[0].wait()
    enter(su, lambda at: state[0, :, at])
    enter(sv, lambda at: state[1, :, at])
    enter(sx, lambda at: state[2, :, at])
    enter(sy, lambda at: state[3, :, at])
    enter(sxy, lambda at: state[4, :, at])
    for copy in copies[1:]:
        copy.wait()
    enter(cp, lambda at: strength[:, at])
    enter(ca, lambda at: mass[:, at])
    enter(gx, lambda at: wind[0, :, at] + surface[0, :, at])
    enter(gy, lambda at: wind[1, :, at] + surface[1, :, at])

    lane = lane_index(pairs)
    final = (lane & (BX // 2 - 1)) == BX // 2 - 1
    initial = (lane & (BX // 2 - 1)) == 0

    def ahead(even, odd):
        return (
            odd - even,
            jnp.where(final, 0.0, pltpu.roll(even, LANES - 1, axis=1) - odd),
        )

    def behind(even, odd):
        return (
            even - jnp.where(initial, 0.0, pltpu.roll(odd, 1, axis=1)),
            odd - even,
        )

    def vec(odd, y):
        return pl.ds(odd * area + y * pairs, pairs)

    def row_of(ref, y):
        return (ref[vec(0, y), :], ref[vec(1, y), :])

    below = None
    for y in range(rows):
        p = tuple(RELAX * s for s in row_of(cp, y))
        across = behind(*p)
        for odd in range(2):
            i = vec(odd, y)
            m = ca[i, :]
            inverse = 1.0 / (m + SUB_STEP)
            push = SUB_STEP * inverse
            down = p[odd] if y == 0 else p[odd] - below[odd]
            gx[i, :] = push * (gx[i, :] - across[odd])
            gy[i, :] = push * (gy[i, :] - down)
            ca[i, :] = m * inverse
            cb[i, :] = push
            cq[i, :] = p[odd] * (0.625 * DECAY / 1.25**0.5)
            cp[i, :] = p[odd]
            sx[i, :] = sx[i, :] + p[odd]
            sy[i, :] = sy[i, :] + p[odd]
        below = p

    def sweep(step, carry):
        for _ in range(UNROLL):
            u, v = row_of(su, 0), row_of(sv, 0)
            above = None
            for y in range(rows):
                ux, vx = ahead(*u), ahead(*v)
                xx, yy, xy = [], [], []
                if y < rows - 1:
                    un, vn = row_of(su, y + 1), row_of(sv, y + 1)
                for odd in range(2):
                    i = vec(odd, y)
                    shear = vx[odd]
                    if y < rows - 1:
                        vy = vn[odd] - v[odd]
                        shear = shear + (un[odd] - u[odd])
                        a = ux[odd] + 0.6 * vy
                        b = 0.6 * ux[odd] + vy
                        d = ux[odd] * a + vy * b
                    else:
                        a = ux[odd]
                        b = 0.6 * a
                        d = a * a
                    small = 0.2 * shear
                    q = cq[i, :] * lax.rsqrt(d + (shear * small + 0.2))
                    xx.append(DECAY * sx[i, :] + q * a)
                    yy.append(DECAY * sy[i, :] + q * b)
                    xy.append(DECAY * sxy[i, :] + q * small)
                fx, fy = behind(*xx), behind(*xy)
                for odd in range(2):
                    i = vec(odd, y)
                    sx[i, :] = xx[odd]
                    sy[i, :] = yy[odd]
                    sxy[i, :] = xy[odd]
                    if y:
                        fxo = fx[odd] + (xy[odd] - above[0][odd])
                        fyo = fy[odd] + (yy[odd] - above[1][odd])
                    else:
                        fxo = fx[odd] + xy[odd]
                        fyo = fy[odd] + yy[odd]
                    a0 = ca[i, :]
                    b0 = cb[i, :]
                    uo, vo = u[odd], v[odd]
                    su[i, :] = a0 * (uo + TURNING * SUB_STEP * vo) + (b0 * fxo + gx[i, :])
                    sv[i, :] = a0 * (vo - TURNING * SUB_STEP * uo) + (b0 * fyo + gy[i, :])
                above = (xy, yy)
                if y < rows - 1:
                    u, v = un, vn
        return carry

    lax.fori_loop(0, SUBCYCLES // UNROLL, sweep, 0)

    sx[...] = sx[...] - cp[...]
    sy[...] = sy[...] - cp[...]
    for n, ref in enumerate((su, sv, sx, sy, sxy)):
        value = leave(ref)
        for b in range(blocks):
            at = slice(b * BX, (b + 1) * BX)
            new = value[(b // 2) * rows : (b // 2 + 1) * rows, (b % 2) * BX : (b % 2 + 1) * BX]
            keep = covered[b] == 1
            ice_out[n, :, at] = jnp.where(keep, new, state[n, :, at])
            if n < 2:
                part = fraction[:, at]
                w = wind[n, :, at]
                merged = part * (new - surface[n, :, at]) + (1.0 - part) * w
                stress_out[n, :, at] = jnp.where(keep, merged, w)


def ice(ice_state, strength, ice_mass, ice_fraction, wind_stress, ice_count, ice_list, ocean_state, forward, backward):
    rows, width = ice_mass.shape
    f32 = jnp.float32
    cells = (rows * width // BX, BX)
    return pl.pallas_call(
        ice_kernel,
        name="ice_subcycles",
        out_shape=(
            jax.ShapeDtypeStruct(ice_state.shape, f32),
            jax.ShapeDtypeStruct(wind_stress.shape, f32),
        ),
        in_specs=[spec(SMEM)] * 2 + [spec(HBM)] * 6 + [spec(VMEM)] * 2,
        out_specs=(spec(VMEM), spec(VMEM)),
        scratch_shapes=[
            pltpu.VMEM(ice_state.shape, f32),
            pltpu.VMEM((rows, width), f32),
            pltpu.VMEM((rows, width), f32),
            pltpu.VMEM((rows, width), f32),
            pltpu.VMEM((2, rows, width), f32),
            pltpu.VMEM((2, rows, width), f32),
            pltpu.SemaphoreType.DMA((7,)),
            pltpu.SMEM((width // BX,), jnp.int32),
        ]
        + [pltpu.VMEM(cells, f32)] * 11,
        compiler_params=pltpu.CompilerParams(vmem_limit_bytes=VMEM_BYTES),
        cost_estimate=cost(SUBCYCLES * 50 * rows * width, 4 * 22 * rows * width),
    )(
        ice_count,
        ice_list,
        ice_state,
        strength,
        ice_mass,
        ice_fraction,
        wind_stress,
        ocean_state,
        forward,
        backward,
    )


def main_kernel(
    x_hbm, cols, bih, prev, cor, matrix, mixing, out_hbm, x, out, y, z, in_sem, out_sem
):
    fields, rows, levels, width = x.shape
    steps = width // WIDE
    spans = width // FETCH
    each = FETCH // WIDE

    def fetches(s):
        at = slice(s * FETCH, (s + 1) * FETCH)
        return [
            pltpu.make_async_copy(x_hbm.at[:, :, r, at], x.at[:, r, :, at], in_sem.at[s, r])
            for r in range(rows)
        ]

    def stores(s):
        at = slice(s * FETCH, (s + 1) * FETCH)
        return [
            pltpu.make_async_copy(out.at[:, r, :, at], out_hbm.at[:, :, r, at], out_sem.at[s, r])
            for r in range(rows)
        ]

    for s in range(spans):
        for copy in fetches(s):
            copy.start()

    level = lax.broadcasted_iota(jnp.int32, (HALF, WIDE), 0)
    lane = lax.broadcasted_iota(jnp.int32, (rows * levels, LANES), 1)

    def merge(value):
        return value.reshape(rows * levels, value.shape[-1])

    waited = 0
    for m in range(steps):
        need = min((m + 1) // each, spans - 1)
        while waited <= need:
            for copy in fetches(waited):
                copy.wait()
            waited += 1
        at = slice(m * WIDE, (m + 1) * WIDE)
        for f in range(fields):
            slot = (m * fields + f) % 2
            own = merge(x[f, :, :, at])
            if m == 0:
                west = merge(cols[f])
            else:
                west = merge(x[f, :, :, m * WIDE - LANES : m * WIDE])
            if m == steps - 1:
                east = merge(cols[f])
            else:
                east = merge(x[f, :, :, (m + 1) * WIDE : (m + 1) * WIDE + LANES])
            side = jnp.where(lane < LANES // 2, east, west)
            parts = split(own, 2)
            y[slot] = jnp.dot(
                jnp.concatenate(parts + split(side, 2), axis=1),
                matrix[...],
                preferred_element_type=jnp.float32,
            )
            height = GROUP * levels
            for n in range(rows // GROUP):
                group = slice(n * height, (n + 1) * height)
                z[slot, group, :] = jnp.dot(
                    mixing[...],
                    jnp.concatenate([part[group] for part in parts], axis=0),
                    preferred_element_type=jnp.float32,
                )

            def near(r):
                return y[slot, r * levels : (r + 1) * levels, WIDE : 2 * WIDE]

            for r in range(rows):
                q = x[f, r, :, at]
                lap = y[slot, r * levels : (r + 1) * levels, 0:WIDE]
                for step in (-1, 1):
                    if 0 <= r + step < rows:
                        lap = lap + near(r + step)
                    if 0 <= r + 2 * step < rows:
                        lap = lap + x[f, r + 2 * step, :, at]
                mixed = z[slot, r * levels : (r + 1) * levels, :]
                res = q + KV_MIX * mixed - bih[r : r + 1, at] * lap
                if f == 0:
                    res = res + cor[r] * x[1, r, :, at]
                elif f == 1:
                    res = res - cor[r] * x[0, r, :, at]
                out[f, r, :, at] = res
                if f < 2:
                    out[f, r, 0:HALF, at] = res[0:HALF] + jnp.where(
                        level == 0, prev[f, r : r + 1, at], 0.0
                    )
        if m % each == each - 1:
            for copy in stores(m // each):
                copy.start()
    for s in range(spans):
        for copy in stores(s):
            copy.wait()


def ocean(ocean_state, cols, biharmonic, prev_stress, coriolis, matrix, mixing):
    fields, levels, rows, width = ocean_state.shape
    f32 = jnp.float32
    held = (fields, rows, levels, width)
    return pl.pallas_call(
        main_kernel,
        name="ocean_tile",
        out_shape=jax.ShapeDtypeStruct(ocean_state.shape, f32),
        in_specs=[spec(HBM)] + [spec(VMEM)] * 3 + [spec(SMEM)] + [spec(VMEM)] * 2,
        out_specs=spec(HBM),
        scratch_shapes=[
            pltpu.VMEM(held, f32),
            pltpu.VMEM(held, f32),
            pltpu.VMEM((2, rows * levels, 2 * WIDE), f32),
            pltpu.VMEM((2, rows * levels, WIDE), f32),
            pltpu.SemaphoreType.DMA((width // FETCH, rows)),
            pltpu.SemaphoreType.DMA((width // FETCH, rows)),
        ],
        compiler_params=pltpu.CompilerParams(vmem_limit_bytes=VMEM_BYTES),
        cost_estimate=cost(30 * ocean_state.size, 8 * ocean_state.size),
    )(ocean_state, cols, biharmonic, prev_stress, coriolis, matrix, mixing)


def ends_kernel(above, below, out):
    width = above.shape[3]
    lane = lax.broadcasted_iota(jnp.int32, out.shape[2:], 1)
    for n, (halo, near) in enumerate(((above, 1), (below, 0))):
        for f in range(above.shape[1]):
            out[n, f] = jnp.where(
                lane < LANES // 2,
                halo[near, f, :, 0:LANES],
                halo[near, f, :, width - LANES : width],
            )


def ends(above, below):
    _, fields, levels, _ = above.shape
    return pl.pallas_call(
        ends_kernel,
        name="received_ends",
        out_shape=jax.ShapeDtypeStruct((2, fields, levels, LANES), jnp.float32),
        in_specs=[spec(VMEM)] * 2,
        out_specs=spec(VMEM),
        compiler_params=pltpu.CompilerParams(vmem_limit_bytes=VMEM_BYTES),
    )(above, below)


def fix_kernel(base, above, below, corners, bih, matrix, out, oa, ob, y, in_sem, out_sem):
    _, fields, levels, width = above.shape
    rows = base.shape[2]
    steps = width // WIDE
    fetches, stores = [], []
    for f in range(fields):
        mine, back = [], []
        for j in range(2):
            for side, (buf, first) in enumerate(((oa, 0), (ob, rows - 2))):
                n = (f * 2 + j) * 2 + side
                mine.append(
                    pltpu.make_async_copy(base.at[f, :, first + j, :], buf.at[f, j], in_sem.at[n])
                )
                back.append(
                    pltpu.make_async_copy(buf.at[f, j], out.at[f, :, first + j, :], out_sem.at[n])
                )
        fetches.append(mine)
        stores.append(back)
        for copy in mine:
            copy.start()

    sides = ((above, 1), (below, 0))
    height = 2 * fields * levels
    lane = lax.broadcasted_iota(jnp.int32, (height, LANES), 1)

    def nearest(start, size):
        at = slice(start, start + size)
        return jnp.concatenate(
            [halo[near, f, :, at] for f in range(fields) for halo, near in sides], axis=0
        )

    ends = jnp.concatenate([corners[n, f] for f in range(fields) for n in range(2)], axis=0)
    for m in range(steps):
        west = ends if m == 0 else nearest(m * WIDE - LANES, LANES)
        east = ends if m == steps - 1 else nearest((m + 1) * WIDE, LANES)
        own = nearest(m * WIDE, WIDE)
        side = jnp.where(lane < LANES // 2, east, west)
        y[:, m * WIDE : (m + 1) * WIDE] = jnp.dot(
            jnp.concatenate(split(own, 2) + split(side, 2), axis=1),
            matrix[:, WIDE : 2 * WIDE],
            preferred_element_type=jnp.float32,
        )

    for f in range(fields):
        for copy in fetches[f]:
            copy.wait()
        for n, (halo, near, buf, n1, first) in enumerate(
            ((above, 1, oa, 0, 0), (below, 0, ob, 1, rows - 2))
        ):
            n2 = 1 - n1
            start = (2 * f + n) * levels
            for m in range(steps):
                at = slice(m * WIDE, (m + 1) * WIDE)
                lap = halo[1 - near, f, :, at] + y[start : start + levels, at]
                b1 = bih[first + n1 : first + n1 + 1, at]
                b2 = bih[first + n2 : first + n2 + 1, at]
                buf[f, n1, :, at] = buf[f, n1, :, at] - b1 * lap
                buf[f, n2, :, at] = buf[f, n2, :, at] - b2 * halo[near, f, :, at]
        for copy in stores[f]:
            copy.start()
    for back in stores:
        for copy in back:
            copy.wait()


def fix(base, above, below, corners, biharmonic, matrix):
    fields, levels, rows, width = base.shape
    f32 = jnp.float32
    edge = pltpu.VMEM((fields, 2, levels, width), f32)
    return pl.pallas_call(
        fix_kernel,
        name="ocean_edges",
        out_shape=jax.ShapeDtypeStruct(base.shape, f32),
        in_specs=[spec(HBM)] + [spec(VMEM)] * 5,
        out_specs=spec(HBM),
        input_output_aliases={0: 0},
        scratch_shapes=[
            edge,
            edge,
            pltpu.VMEM((2 * fields * levels, width), f32),
            pltpu.SemaphoreType.DMA((4 * fields,)),
            pltpu.SemaphoreType.DMA((4 * fields,)),
        ],
        compiler_params=pltpu.CompilerParams(vmem_limit_bytes=VMEM_BYTES),
        cost_estimate=cost(0, 3 * 4 * 4 * fields * levels * width),
    )(base, above, below, corners, biharmonic, matrix)


def per_device(
    ocean_state,
    biharmonic,
    prev_stress,
    ice_state,
    strength,
    ice_mass,
    ice_fraction,
    wind_stress,
    ice_count,
    ice_list,
):
    tile_rows = ocean_state.shape[2]
    n_tile = lax.axis_size("tile")
    n_grp = lax.axis_size("grp")

    first, last, cols, matrix, mixing, forward, backward = pack(ocean_state)

    def shift(value, tile_step, grp_step):
        pairs = []
        for g in range(n_grp):
            for t in range(n_tile):
                if 0 <= t + tile_step < n_tile:
                    target = (g + grp_step) % n_grp
                    pairs.append((g * n_tile + t, target * n_tile + t + tile_step))
        return lax.ppermute(value, ("grp", "tile"), pairs)

    def around(value):
        west = shift(value, 0, 1)
        if n_grp == 2:
            return west
        return jnp.where(jnp.arange(LANES) < LANES // 2, shift(value, 0, -1), west)

    above = shift(last, 1, 0)
    below = shift(first, -1, 0)
    cols = around(cols)

    ice_in = (ice_state, strength, ice_mass, ice_fraction, wind_stress, ice_count, ice_list)
    ice_out, stress_out = ice(*ice_in, ocean_state, forward, backward)

    rows = (lax.axis_index("tile") * tile_rows + jnp.arange(tile_rows)).astype(jnp.float32) + 0.5
    coriolis = CORIOLIS * (2.0 * rows / (tile_rows * n_tile) - 1.0)

    above, below, ice_out, stress_out = lax.optimization_barrier(
        (above, below, ice_out, stress_out)
    )

    corners = ends(above, below)
    corners, cols = lax.optimization_barrier((corners, cols))
    corners = around(corners)

    base = ocean(ocean_state, cols, biharmonic, prev_stress, coriolis, matrix, mixing)
    ocean_out = fix(base, above, below, corners, biharmonic, matrix)
    return (ocean_out, ice_out, stress_out)


def solution(mesh):
    placed = (
        P(None, None, "tile", "grp"),
        P("tile", "grp"),
        P(None, "tile", "grp"),
        P(None, "tile", "grp"),
        P("tile", "grp"),
        P("tile", "grp"),
        P("tile", "grp"),
        P(None, "tile", "grp"),
        P(("grp", "tile")),
        P(("grp", "tile"), None),
    )
    return jax.shard_map(
        per_device,
        mesh=mesh,
        in_specs=placed,
        out_specs=(P(None, None, "tile", "grp"), P(None, "tile", "grp"), P(None, "tile", "grp")),
        check_vma=False,
    )
```

```python
import jax
import jax.numpy as jnp
from jax import lax
from jax.experimental import pallas as pl
from jax.experimental.pallas import tpu as pltpu
from jax.sharding import PartitionSpec as P

BY = 16
BX = 128
SUBCYCLES = 64
UNROLL = 4
LANES = 128
HALF = 8

KV_MIX = 0.2
RELAX = 0.5
SUB_STEP = 0.3
TURNING = 0.3
CORIOLIS = 0.2

DECAY = 1.0 / (1.0 + RELAX)
VMEM_BYTES = 48 * 1024 * 1024
SMALL_BYTES = 24 * 1024 * 1024

HBM = pltpu.HBM
VMEM = pltpu.VMEM
SMEM = pltpu.SMEM


def spec(space):
    return pl.BlockSpec(memory_space=space)


def cost(flops, nbytes):
    return pl.CostEstimate(flops=flops, bytes_accessed=nbytes, transcendentals=0)


def lane_index(rows):
    return lax.broadcasted_iota(jnp.int32, (rows, LANES), 1)


WIDE = 256
GROUP = 4


def iota(shape, dim):
    return lax.broadcasted_iota(jnp.int32, shape, dim)


def as_matrix(value):
    return value.astype(jnp.float32).astype(jnp.bfloat16)


def column_taps(source, shape):
    place = iota(shape, 1)
    d = jnp.abs(source - (place & (WIDE - 1)))
    double = jnp.where(d == 0, 20, jnp.where(d == 1, -8, jnp.where(d == 2, 1, 0)))
    single = jnp.where(d == 0, -8, jnp.where(d == 1, 2, 0))
    return as_matrix(jnp.where(place < WIDE, double, single))


def make_columns(matrix):
    own = (WIDE, 2 * WIDE)
    taps = column_taps(iota(own, 0), own)
    matrix[0:WIDE, :] = taps
    matrix[WIDE : 2 * WIDE, :] = taps
    side = (LANES, 2 * WIDE)
    lane = iota(side, 0)
    taps = column_taps(jnp.where(lane < LANES // 2, lane + WIDE, lane - LANES), side)
    matrix[2 * WIDE : 2 * WIDE + LANES, :] = taps
    matrix[2 * WIDE + LANES : 2 * WIDE + 2 * LANES, :] = taps


def make_mixing(mixing, levels):
    height = GROUP * levels
    shape = mixing.shape
    a, c = iota(shape, 0), iota(shape, 1)
    c = jnp.where(c >= height, c - height, c)

    def parts(index):
        group = jnp.zeros(shape, jnp.int32)
        for n in range(1, GROUP):
            group = group + jnp.where(index >= n * levels, 1, 0)
        return group, index - levels * group

    ga, la = parts(a)
    gc, lc = parts(c)
    value = (
        jnp.where(lc == jnp.maximum(la - 1, 0), 1, 0)
        + jnp.where(lc == jnp.minimum(la + 1, levels - 1), 1, 0)
        - jnp.where(lc == la, 2, 0)
    )
    mixing[...] = as_matrix(jnp.where(ga == gc, value, 0))


def make_orders(forward, backward):
    shape = forward.shape

    def target(i):
        return ((i & 1) * BX) + ((i >> 7) * (BX // 2)) + ((i & (BX - 1)) >> 1)

    forward[...] = as_matrix(jnp.where(target(iota(shape, 0)) == iota(shape, 1), 1, 0))
    backward[...] = as_matrix(jnp.where(target(iota(shape, 1)) == iota(shape, 0), 1, 0))


def pack_kernel(
    x,
    flat,
    first,
    last,
    cols,
    left,
    right,
    row_sem,
    col_sem,
):
    rows, width = x.shape[2:]
    copies = []
    for j in range(2):
        for side, (to, row) in enumerate(((first, j), (last, rows - 2 + j))):
            copies.append(
                pltpu.make_async_copy(x.at[:, :, row, :], to.at[j], row_sem.at[side, j])
            )
    col_copies = [
        pltpu.make_async_copy(flat.at[:, :, start : start + LANES], to, col_sem.at[side])
        for side, (to, start) in enumerate(((left, 0), (right, width - LANES)))
    ]
    for copy in copies + col_copies:
        copy.start()
    for copy in col_copies:
        copy.wait()
    lane = lax.broadcasted_iota(jnp.int32, cols.shape[2:], 1)
    levels = x.shape[1]
    for f in range(left.shape[0]):
        for r in range(rows):
            at = pl.ds(r, levels, stride=rows)
            cols[f, r] = jnp.where(lane < LANES // 2, left[f, at, :], right[f, at, :])
    for copy in copies:
        copy.wait()


def flatten(array):
    fields, levels, rows, width = array.shape
    return array.reshape(fields, levels * rows, width)


def pack(ocean_state):
    fields, levels, rows, width = ocean_state.shape
    f32 = jnp.float32
    edge = (fields, rows, levels, LANES)
    return pl.pallas_call(
        pack_kernel,
        name="pack_edges",
        out_shape=(
            jax.ShapeDtypeStruct((2, fields, levels, width), f32),
            jax.ShapeDtypeStruct((2, fields, levels, width), f32),
            jax.ShapeDtypeStruct(edge, f32),
        ),
        in_specs=[spec(HBM)] * 2,
        out_specs=(spec(VMEM),) * 3,
        scratch_shapes=[
            pltpu.VMEM((fields, levels * rows, LANES), f32),
            pltpu.VMEM((fields, levels * rows, LANES), f32),
            pltpu.SemaphoreType.DMA((2, 2)),
            pltpu.SemaphoreType.DMA((2,)),
        ],
        compiler_params=pltpu.CompilerParams(vmem_limit_bytes=VMEM_BYTES),
        cost_estimate=cost(0, 4 * 2 * 4 * fields * levels * width),
    )(ocean_state, flatten(ocean_state))


def split(q, parts):
    out = []
    for _ in range(parts):
        part = q.astype(jnp.bfloat16)
        out.append(part)
        q = q - part.astype(jnp.float32)
    return out


def reorder(value, matrix):
    total = None
    for part in split(value, 3):
        term = jnp.dot(part, matrix, preferred_element_type=jnp.float32)
        total = term if total is None else total + term
    return total


def ice_kernel(
    count,
    listed,
    state_hbm,
    strength_hbm,
    mass_hbm,
    fraction_hbm,
    wind_hbm,
    ocean_hbm,
    ice_out,
    stress_out,
    forward,
    backward,
    state,
    strength,
    mass,
    fraction,
    wind,
    surface,
    sem,
    covered,
    su,
    sv,
    sx,
    sy,
    sxy,
    cp,
    cq,
    ca,
    cb,
    gx,
    gy,
):
    rows, width = mass.shape
    wide = 2 * BX
    pairs = width // wide
    area = rows * pairs
    blocks = width // BX

    copies = [
        pltpu.make_async_copy(source, to, sem.at[n])
        for n, (source, to) in enumerate(
            (
                (state_hbm, state),
                (strength_hbm, strength),
                (mass_hbm, mass),
                (wind_hbm, wind),
                (ocean_hbm.at[0, 0], surface.at[0]),
                (ocean_hbm.at[1, 0], surface.at[1]),
                (fraction_hbm, fraction),
            )
        )
    ]
    for copy in copies:
        copy.start()

    make_orders(forward, backward)
    for s in range(blocks):
        covered[listed[0, s]] = jnp.where(s < count[0], 1, 0)

    def chunk(j):
        return slice(j * wide, (j + 1) * wide)

    def place(j, odd):
        return pl.ds(odd * area + j, rows, stride=pairs)

    def enter(ref, get):
        value = jnp.concatenate([get(chunk(j)) for j in range(pairs)], axis=0)
        value = reorder(value, forward[...])
        for j in range(pairs):
            for odd in range(2):
                ref[place(j, odd), :] = value[
                    j * rows : (j + 1) * rows, odd * BX : (odd + 1) * BX
                ]

    def leave(ref):
        value = jnp.concatenate(
            [
                jnp.concatenate([ref[place(j, 0), :], ref[place(j, 1), :]], axis=1)
                for j in range(pairs)
            ],
            axis=0,
        )
        return reorder(value, backward[...])

    copies[0].wait()
    enter(su, lambda at: state[0, :, at])
    enter(sv, lambda at: state[1, :, at])
    enter(sx, lambda at: state[2, :, at])
    enter(sy, lambda at: state[3, :, at])
    enter(sxy, lambda at: state[4, :, at])
    for copy in copies[1:]:
        copy.wait()
    enter(cp, lambda at: strength[:, at])
    enter(ca, lambda at: mass[:, at])
    enter(gx, lambda at: wind[0, :, at] + surface[0, :, at])
    enter(gy, lambda at: wind[1, :, at] + surface[1, :, at])

    lane = lane_index(pairs)
    final = (lane & (BX // 2 - 1)) == BX // 2 - 1
    initial = (lane & (BX // 2 - 1)) == 0

    def ahead(even, odd):
        return (
            odd - even,
            jnp.where(final, 0.0, pltpu.roll(even, LANES - 1, axis=1) - odd),
        )

    def behind(even, odd):
        return (
            even - jnp.where(initial, 0.0, pltpu.roll(odd, 1, axis=1)),
            odd - even,
        )

    def vec(odd, y):
        return pl.ds(odd * area + y * pairs, pairs)

    def row_of(ref, y):
        return (ref[vec(0, y), :], ref[vec(1, y), :])

    below = None
    for y in range(rows):
        p = tuple(RELAX * s for s in row_of(cp, y))
        across = behind(*p)
        for odd in range(2):
            i = vec(odd, y)
            m = ca[i, :]
            inverse = 1.0 / (m + SUB_STEP)
            push = SUB_STEP * inverse
            down = p[odd] if y == 0 else p[odd] - below[odd]
            gx[i, :] = push * (gx[i, :] - across[odd])
            gy[i, :] = push * (gy[i, :] - down)
            ca[i, :] = m * inverse
            cb[i, :] = push
            cq[i, :] = p[odd] * (0.625 * DECAY / 1.25**0.5)
            cp[i, :] = p[odd]
            sx[i, :] = sx[i, :] + p[odd]
            sy[i, :] = sy[i, :] + p[odd]
        below = p

    def sweep(step, carry):
        for _ in range(UNROLL):
            u, v = row_of(su, 0), row_of(sv, 0)
            above = None
            for y in range(rows):
                ux, vx = ahead(*u), ahead(*v)
                xx, yy, xy = [], [], []
                if y < rows - 1:
                    un, vn = row_of(su, y + 1), row_of(sv, y + 1)
                for odd in range(2):
                    i = vec(odd, y)
                    shear = vx[odd]
                    if y < rows - 1:
                        vy = vn[odd] - v[odd]
                        shear = shear + (un[odd] - u[odd])
                        a = ux[odd] + 0.6 * vy
                        b = 0.6 * ux[odd] + vy
                        d = ux[odd] * a + vy * b
                    else:
                        a = ux[odd]
                        b = 0.6 * a
                        d = a * a
                    small = 0.2 * shear
                    q = cq[i, :] * lax.rsqrt(d + (shear * small + 0.2))
                    xx.append(DECAY * sx[i, :] + q * a)
                    yy.append(DECAY * sy[i, :] + q * b)
                    xy.append(DECAY * sxy[i, :] + q * small)
                fx, fy = behind(*xx), behind(*xy)
                for odd in range(2):
                    i = vec(odd, y)
                    sx[i, :] = xx[odd]
                    sy[i, :] = yy[odd]
                    sxy[i, :] = xy[odd]
                    if y:
                        fxo = fx[odd] + (xy[odd] - above[0][odd])
                        fyo = fy[odd] + (yy[odd] - above[1][odd])
                    else:
                        fxo = fx[odd] + xy[odd]
                        fyo = fy[odd] + yy[odd]
                    a0 = ca[i, :]
                    b0 = cb[i, :]
                    uo, vo = u[odd], v[odd]
                    su[i, :] = a0 * (uo + TURNING * SUB_STEP * vo) + (b0 * fxo + gx[i, :])
                    sv[i, :] = a0 * (vo - TURNING * SUB_STEP * uo) + (b0 * fyo + gy[i, :])
                above = (xy, yy)
                if y < rows - 1:
                    u, v = un, vn
        return carry

    lax.fori_loop(0, SUBCYCLES // UNROLL, sweep, 0)

    sx[...] = sx[...] - cp[...]
    sy[...] = sy[...] - cp[...]
    for n, ref in enumerate((su, sv, sx, sy, sxy)):
        value = leave(ref)
        for b in range(blocks):
            at = slice(b * BX, (b + 1) * BX)
            new = value[(b // 2) * rows : (b // 2 + 1) * rows, (b % 2) * BX : (b % 2 + 1) * BX]
            keep = covered[b] == 1
            ice_out[n, :, at] = jnp.where(keep, new, state[n, :, at])
            if n < 2:
                part = fraction[:, at]
                w = wind[n, :, at]
                merged = part * (new - surface[n, :, at]) + (1.0 - part) * w
                stress_out[n, :, at] = jnp.where(keep, merged, w)


def ice(ice_state, strength, ice_mass, ice_fraction, wind_stress, ice_count, ice_list, ocean_state):
    rows, width = ice_mass.shape
    f32 = jnp.float32
    cells = (rows * width // BX, BX)
    return pl.pallas_call(
        ice_kernel,
        name="ice_subcycles",
        out_shape=(
            jax.ShapeDtypeStruct(ice_state.shape, f32),
            jax.ShapeDtypeStruct(wind_stress.shape, f32),
        ),
        in_specs=[spec(SMEM)] * 2 + [spec(HBM)] * 6,
        out_specs=(spec(VMEM), spec(VMEM)),
        scratch_shapes=[
            pltpu.VMEM((2 * BX, 2 * BX), jnp.bfloat16),
            pltpu.VMEM((2 * BX, 2 * BX), jnp.bfloat16),
            pltpu.VMEM(ice_state.shape, f32),
            pltpu.VMEM((rows, width), f32),
            pltpu.VMEM((rows, width), f32),
            pltpu.VMEM((rows, width), f32),
            pltpu.VMEM((2, rows, width), f32),
            pltpu.VMEM((2, rows, width), f32),
            pltpu.SemaphoreType.DMA((7,)),
            pltpu.SMEM((width // BX,), jnp.int32),
        ]
        + [pltpu.VMEM(cells, f32)] * 11,
        compiler_params=pltpu.CompilerParams(vmem_limit_bytes=VMEM_BYTES),
        cost_estimate=cost(SUBCYCLES * 50 * rows * width, 4 * 22 * rows * width),
    )(
        ice_count,
        ice_list,
        ice_state,
        strength,
        ice_mass,
        ice_fraction,
        wind_stress,
        ocean_state,
    )


def main_kernel(
    x_hbm,
    cols,
    bih,
    prev,
    cor,
    out_hbm,
    x,
    raw,
    out,
    y,
    z,
    matrix,
    mixing,
    in_sem,
    out_sem,
):
    fields, rows, levels, width = x.shape
    steps = width // WIDE
    tiles = width // LANES
    each = WIDE // LANES

    def fetch(c):
        at = slice(c * LANES, (c + 1) * LANES)
        return pltpu.make_async_copy(x_hbm.at[:, :, at], raw.at[:, c], in_sem.at[c])

    def store(c):
        at = slice(c * LANES, (c + 1) * LANES)
        return pltpu.make_async_copy(out.at[:, c], out_hbm.at[:, :, at], out_sem.at[c])

    for c in range(tiles):
        fetch(c).start()
    make_columns(matrix)
    make_mixing(mixing, levels)

    level = lax.broadcasted_iota(jnp.int32, (HALF, WIDE), 0)
    lane = lax.broadcasted_iota(jnp.int32, (rows * levels, LANES), 1)

    def merge(value):
        return value.reshape(rows * levels, value.shape[-1])

    waited = 0
    for m in range(steps):
        while waited < min((m + 1) * each + 1, tiles):
            fetch(waited).wait()
            to = slice(waited * LANES, (waited + 1) * LANES)
            for f in range(fields):
                for r in range(rows):
                    x[f, r, :, to] = raw[f, waited, pl.ds(r, levels, stride=rows), :]
            waited += 1
        at = slice(m * WIDE, (m + 1) * WIDE)
        for f in range(fields):
            slot = (m * fields + f) % 2
            own = merge(x[f, :, :, at])
            if m == 0:
                west = merge(cols[f])
            else:
                west = merge(x[f, :, :, m * WIDE - LANES : m * WIDE])
            if m == steps - 1:
                east = merge(cols[f])
            else:
                east = merge(x[f, :, :, (m + 1) * WIDE : (m + 1) * WIDE + LANES])
            side = jnp.where(lane < LANES // 2, east, west)
            parts = split(own, 2)
            y[slot] = jnp.dot(
                jnp.concatenate(parts + split(side, 2), axis=1),
                matrix[...],
                preferred_element_type=jnp.float32,
            )
            height = GROUP * levels
            for n in range(rows // GROUP):
                group = slice(n * height, (n + 1) * height)
                z[slot, group, :] = jnp.dot(
                    mixing[...],
                    jnp.concatenate([part[group] for part in parts], axis=0),
                    preferred_element_type=jnp.float32,
                )

            def near(r):
                return y[slot, r * levels : (r + 1) * levels, WIDE : 2 * WIDE]

            for r in range(rows):
                q = x[f, r, :, at]
                lap = y[slot, r * levels : (r + 1) * levels, 0:WIDE]
                for step in (-1, 1):
                    if 0 <= r + step < rows:
                        lap = lap + near(r + step)
                    if 0 <= r + 2 * step < rows:
                        lap = lap + x[f, r + 2 * step, :, at]
                mixed = z[slot, r * levels : (r + 1) * levels, :]
                res = q + KV_MIX * mixed - bih[r : r + 1, at] * lap
                if f == 0:
                    res = res + cor[r] * x[1, r, :, at]
                elif f == 1:
                    res = res - cor[r] * x[0, r, :, at]
                if f < 2:
                    head = res[0:HALF] + jnp.where(level == 0, prev[f, r : r + 1, at], 0.0)
                    res = jnp.concatenate([head, res[HALF:]], axis=0)
                for n in range(each):
                    out[f, m * each + n, pl.ds(r, levels, stride=rows), :] = res[
                        :, n * LANES : (n + 1) * LANES
                    ]
        for n in range(each):
            store(m * each + n).start()
    for c in range(tiles):
        store(c).wait()


def ocean(ocean_state, cols, biharmonic, prev_stress, coriolis):
    fields, levels, rows, width = ocean_state.shape
    f32 = jnp.float32
    tiled = (fields, width // LANES, levels * rows, LANES)
    base = pl.pallas_call(
        main_kernel,
        name="ocean_tile",
        out_shape=jax.ShapeDtypeStruct((fields, levels * rows, width), f32),
        in_specs=[spec(HBM)] + [spec(VMEM)] * 3 + [spec(SMEM)],
        out_specs=spec(HBM),
        scratch_shapes=[
            pltpu.VMEM((fields, rows, levels, width), f32),
            pltpu.VMEM(tiled, f32),
            pltpu.VMEM(tiled, f32),
            pltpu.VMEM((2, rows * levels, 2 * WIDE), f32),
            pltpu.VMEM((2, rows * levels, WIDE), f32),
            pltpu.VMEM((2 * (WIDE + LANES), 2 * WIDE), jnp.bfloat16),
            pltpu.VMEM((GROUP * levels, 2 * GROUP * levels), jnp.bfloat16),
            pltpu.SemaphoreType.DMA((width // LANES,)),
            pltpu.SemaphoreType.DMA((width // LANES,)),
        ],
        compiler_params=pltpu.CompilerParams(vmem_limit_bytes=VMEM_BYTES),
        cost_estimate=cost(30 * ocean_state.size, 8 * ocean_state.size),
    )(flatten(ocean_state), cols, biharmonic, prev_stress, coriolis)
    return base.reshape(ocean_state.shape)


def ends_kernel(above, below, out):
    width = above.shape[3]
    lane = lax.broadcasted_iota(jnp.int32, out.shape[2:], 1)
    for n, (halo, near) in enumerate(((above, 1), (below, 0))):
        for f in range(above.shape[1]):
            out[n, f] = jnp.where(
                lane < LANES // 2,
                halo[near, f, :, 0:LANES],
                halo[near, f, :, width - LANES : width],
            )


def ends(above, below):
    _, fields, levels, _ = above.shape
    return pl.pallas_call(
        ends_kernel,
        name="received_ends",
        out_shape=jax.ShapeDtypeStruct((2, fields, levels, LANES), jnp.float32),
        in_specs=[spec(VMEM)] * 2,
        out_specs=spec(VMEM),
        compiler_params=pltpu.CompilerParams(vmem_limit_bytes=SMALL_BYTES),
    )(above, below)


def fix_kernel(base, above, below, corners, bih, out, oa, ob, y, matrix, in_sem, out_sem):
    _, fields, levels, width = above.shape
    rows = base.shape[2]
    steps = width // WIDE
    fetches, stores = [], []
    for f in range(fields):
        mine, back = [], []
        for j in range(2):
            for side, (buf, first) in enumerate(((oa, 0), (ob, rows - 2))):
                n = (f * 2 + j) * 2 + side
                mine.append(
                    pltpu.make_async_copy(base.at[f, :, first + j, :], buf.at[f, j], in_sem.at[n])
                )
                back.append(
                    pltpu.make_async_copy(buf.at[f, j], out.at[f, :, first + j, :], out_sem.at[n])
                )
        fetches.append(mine)
        stores.append(back)
        for copy in mine:
            copy.start()

    make_columns(matrix)
    sides = ((above, 1), (below, 0))
    height = 2 * fields * levels
    lane = lax.broadcasted_iota(jnp.int32, (height, LANES), 1)

    def nearest(start, size):
        at = slice(start, start + size)
        return jnp.concatenate(
            [halo[near, f, :, at] for f in range(fields) for halo, near in sides], axis=0
        )

    ends = jnp.concatenate([corners[n, f] for f in range(fields) for n in range(2)], axis=0)
    for m in range(steps):
        west = ends if m == 0 else nearest(m * WIDE - LANES, LANES)
        east = ends if m == steps - 1 else nearest((m + 1) * WIDE, LANES)
        own = nearest(m * WIDE, WIDE)
        side = jnp.where(lane < LANES // 2, east, west)
        y[:, m * WIDE : (m + 1) * WIDE] = jnp.dot(
            jnp.concatenate(split(own, 2) + split(side, 2), axis=1),
            matrix[:, WIDE : 2 * WIDE],
            preferred_element_type=jnp.float32,
        )

    for f in range(fields):
        for copy in fetches[f]:
            copy.wait()
        for n, (halo, near, buf, n1, first) in enumerate(
            ((above, 1, oa, 0, 0), (below, 0, ob, 1, rows - 2))
        ):
            n2 = 1 - n1
            start = (2 * f + n) * levels
            for m in range(steps):
                at = slice(m * WIDE, (m + 1) * WIDE)
                lap = halo[1 - near, f, :, at] + y[start : start + levels, at]
                b1 = bih[first + n1 : first + n1 + 1, at]
                b2 = bih[first + n2 : first + n2 + 1, at]
                buf[f, n1, :, at] = buf[f, n1, :, at] - b1 * lap
                buf[f, n2, :, at] = buf[f, n2, :, at] - b2 * halo[near, f, :, at]
        for copy in stores[f]:
            copy.start()
    for back in stores:
        for copy in back:
            copy.wait()


def fix(base, above, below, corners, biharmonic):
    fields, levels, rows, width = base.shape
    f32 = jnp.float32
    edge = pltpu.VMEM((fields, 2, levels, width), f32)
    return pl.pallas_call(
        fix_kernel,
        name="ocean_edges",
        out_shape=jax.ShapeDtypeStruct(base.shape, f32),
        in_specs=[spec(HBM)] + [spec(VMEM)] * 4,
        out_specs=spec(HBM),
        input_output_aliases={0: 0},
        scratch_shapes=[
            edge,
            edge,
            pltpu.VMEM((2 * fields * levels, width), f32),
            pltpu.VMEM((2 * (WIDE + LANES), 2 * WIDE), jnp.bfloat16),
            pltpu.SemaphoreType.DMA((4 * fields,)),
            pltpu.SemaphoreType.DMA((4 * fields,)),
        ],
        compiler_params=pltpu.CompilerParams(vmem_limit_bytes=SMALL_BYTES),
        cost_estimate=cost(0, 3 * 4 * 4 * fields * levels * width),
    )(base, above, below, corners, biharmonic)


def per_device(
    ocean_state,
    biharmonic,
    prev_stress,
    ice_state,
    strength,
    ice_mass,
    ice_fraction,
    wind_stress,
    ice_count,
    ice_list,
):
    tile_rows = ocean_state.shape[2]
    n_tile = lax.axis_size("tile")
    n_grp = lax.axis_size("grp")

    first, last, cols = pack(ocean_state)

    def shift(value, tile_step, grp_step):
        pairs = []
        for g in range(n_grp):
            for t in range(n_tile):
                if 0 <= t + tile_step < n_tile:
                    target = (g + grp_step) % n_grp
                    pairs.append((g * n_tile + t, target * n_tile + t + tile_step))
        return lax.ppermute(value, ("grp", "tile"), pairs)

    def around(value):
        west = shift(value, 0, 1)
        if n_grp == 2:
            return west
        return jnp.where(jnp.arange(LANES) < LANES // 2, shift(value, 0, -1), west)

    above = shift(last, 1, 0)
    below = shift(first, -1, 0)
    cols = around(cols)

    ice_in = (ice_state, strength, ice_mass, ice_fraction, wind_stress, ice_count, ice_list)
    ice_out, stress_out = ice(*ice_in, ocean_state)

    rows = (lax.axis_index("tile") * tile_rows + jnp.arange(tile_rows)).astype(jnp.float32) + 0.5
    coriolis = CORIOLIS * (2.0 * rows / (tile_rows * n_tile) - 1.0)

    cols, ice_out, stress_out = lax.optimization_barrier((cols, ice_out, stress_out))
    base = ocean(ocean_state, cols, biharmonic, prev_stress, coriolis)

    above, below, base = lax.optimization_barrier((above, below, base))
    corners = around(ends(above, below))
    ocean_out = fix(base, above, below, corners, biharmonic)
    return (ocean_out, ice_out, stress_out)


def solution(mesh):
    placed = (
        P(None, None, "tile", "grp"),
        P("tile", "grp"),
        P(None, "tile", "grp"),
        P(None, "tile", "grp"),
        P("tile", "grp"),
        P("tile", "grp"),
        P("tile", "grp"),
        P(None, "tile", "grp"),
        P(("grp", "tile")),
        P(("grp", "tile"), None),
    )
    return jax.shard_map(
        per_device,
        mesh=mesh,
        in_specs=placed,
        out_specs=(P(None, None, "tile", "grp"), P(None, "tile", "grp"), P(None, "tile", "grp")),
        check_vma=False,
    )
```

```python
import jax
import jax.numpy as jnp
from jax import lax
from jax.experimental import pallas as pl
from jax.experimental.pallas import tpu as pltpu
from jax.sharding import PartitionSpec as P

BY = 16
BX = 128
SUBCYCLES = 64
UNROLL = 4
LANES = 128
HALF = 8

KV_MIX = 0.2
RELAX = 0.5
SUB_STEP = 0.3
TURNING = 0.3
CORIOLIS = 0.2

DECAY = 1.0 / (1.0 + RELAX)
VMEM_BYTES = 48 * 1024 * 1024
SMALL_BYTES = 24 * 1024 * 1024

HBM = pltpu.HBM
VMEM = pltpu.VMEM
SMEM = pltpu.SMEM


def spec(space):
    return pl.BlockSpec(memory_space=space)


def cost(flops, nbytes):
    return pl.CostEstimate(flops=flops, bytes_accessed=nbytes, transcendentals=0)


def lane_index(rows):
    return lax.broadcasted_iota(jnp.int32, (rows, LANES), 1)


WIDE = 256


def iota(shape, dim):
    return lax.broadcasted_iota(jnp.int32, shape, dim)


def as_matrix(value):
    return value.astype(jnp.float32).astype(jnp.bfloat16)


def column_taps(source, shape):
    place = iota(shape, 1)
    wide = shape[1] // 2
    d = jnp.abs(source - (place & (wide - 1)))
    double = jnp.where(d == 0, 20, jnp.where(d == 1, -8, jnp.where(d == 2, 1, 0)))
    single = jnp.where(d == 0, -8, jnp.where(d == 1, 2, 0))
    return as_matrix(jnp.where(place < wide, double, single))


def make_columns(matrix):
    wide = matrix.shape[1] // 2
    own = (wide, 2 * wide)
    taps = column_taps(iota(own, 0), own)
    matrix[0:wide, :] = taps
    matrix[wide : 2 * wide, :] = taps
    side = (LANES, 2 * wide)
    lane = iota(side, 0)
    taps = column_taps(jnp.where(lane < LANES // 2, lane + wide, lane - LANES), side)
    matrix[2 * wide : 2 * wide + LANES, :] = taps
    matrix[2 * wide + LANES : 2 * wide + 2 * LANES, :] = taps


def make_orders(forward, backward):
    shape = forward.shape

    def target(i):
        return ((i & 1) * BX) + ((i >> 7) * (BX // 2)) + ((i & (BX - 1)) >> 1)

    forward[...] = as_matrix(jnp.where(target(iota(shape, 0)) == iota(shape, 1), 1, 0))
    backward[...] = as_matrix(jnp.where(target(iota(shape, 1)) == iota(shape, 0), 1, 0))


def pack_kernel(
    x,
    flat,
    first,
    last,
    cols,
    left,
    right,
    row_sem,
    col_sem,
):
    rows, width = x.shape[2:]
    copies = []
    for j in range(2):
        for side, (to, row) in enumerate(((first, j), (last, rows - 2 + j))):
            copies.append(
                pltpu.make_async_copy(x.at[:, :, row, :], to.at[j], row_sem.at[side, j])
            )
    col_copies = [
        pltpu.make_async_copy(flat.at[:, :, start : start + LANES], to, col_sem.at[side])
        for side, (to, start) in enumerate(((left, 0), (right, width - LANES)))
    ]
    for copy in copies + col_copies:
        copy.start()
    for copy in col_copies:
        copy.wait()
    lane = lax.broadcasted_iota(jnp.int32, cols.shape[2:], 1)
    levels = x.shape[1]
    for f in range(left.shape[0]):
        for r in range(rows):
            at = pl.ds(r, levels, stride=rows)
            cols[f, r] = jnp.where(lane < LANES // 2, left[f, at, :], right[f, at, :])
    for copy in copies:
        copy.wait()


def flatten(array):
    fields, levels, rows, width = array.shape
    return array.reshape(fields, levels * rows, width)


def pack(ocean_state):
    fields, levels, rows, width = ocean_state.shape
    f32 = jnp.float32
    edge = (fields, rows, levels, LANES)
    return pl.pallas_call(
        pack_kernel,
        name="pack_edges",
        out_shape=(
            jax.ShapeDtypeStruct((2, fields, levels, width), f32),
            jax.ShapeDtypeStruct((2, fields, levels, width), f32),
            jax.ShapeDtypeStruct(edge, f32),
        ),
        in_specs=[spec(HBM)] * 2,
        out_specs=(spec(VMEM),) * 3,
        scratch_shapes=[
            pltpu.VMEM((fields, levels * rows, LANES), f32),
            pltpu.VMEM((fields, levels * rows, LANES), f32),
            pltpu.SemaphoreType.DMA((2, 2)),
            pltpu.SemaphoreType.DMA((2,)),
        ],
        compiler_params=pltpu.CompilerParams(vmem_limit_bytes=VMEM_BYTES),
        cost_estimate=cost(0, 4 * 2 * 4 * fields * levels * width),
    )(ocean_state, flatten(ocean_state))


def split(q, parts):
    out = []
    for _ in range(parts):
        part = q.astype(jnp.bfloat16)
        out.append(part)
        q = q - part.astype(jnp.float32)
    return out


def reorder(value, matrix):
    total = None
    for part in split(value, 3):
        term = jnp.dot(part, matrix, preferred_element_type=jnp.float32)
        total = term if total is None else total + term
    return total


def ice_kernel(
    count,
    listed,
    state_hbm,
    strength_hbm,
    mass_hbm,
    fraction_hbm,
    wind_hbm,
    ocean_hbm,
    ice_out,
    stress_out,
    forward,
    backward,
    state,
    strength,
    mass,
    fraction,
    wind,
    surface,
    sem,
    covered,
    su,
    sv,
    sx,
    sy,
    sxy,
    cp,
    cq,
    ca,
    cb,
    gx,
    gy,
):
    rows, width = mass.shape
    wide = 2 * BX
    pairs = width // wide
    area = rows * pairs
    blocks = width // BX

    copies = [
        pltpu.make_async_copy(source, to, sem.at[n])
        for n, (source, to) in enumerate(
            (
                (state_hbm, state),
                (strength_hbm, strength),
                (mass_hbm, mass),
                (wind_hbm, wind),
                (ocean_hbm.at[0, 0], surface.at[0]),
                (ocean_hbm.at[1, 0], surface.at[1]),
                (fraction_hbm, fraction),
            )
        )
    ]
    for copy in copies:
        copy.start()

    make_orders(forward, backward)
    for s in range(blocks):
        covered[listed[0, s]] = jnp.where(s < count[0], 1, 0)

    def chunk(j):
        return slice(j * wide, (j + 1) * wide)

    def place(j, odd):
        return pl.ds(odd * area + j, rows, stride=pairs)

    def enter(ref, get):
        value = jnp.concatenate([get(chunk(j)) for j in range(pairs)], axis=0)
        value = reorder(value, forward[...])
        for j in range(pairs):
            for odd in range(2):
                ref[place(j, odd), :] = value[
                    j * rows : (j + 1) * rows, odd * BX : (odd + 1) * BX
                ]

    def leave(ref):
        value = jnp.concatenate(
            [
                jnp.concatenate([ref[place(j, 0), :], ref[place(j, 1), :]], axis=1)
                for j in range(pairs)
            ],
            axis=0,
        )
        return reorder(value, backward[...])

    copies[0].wait()
    enter(su, lambda at: state[0, :, at])
    enter(sv, lambda at: state[1, :, at])
    enter(sx, lambda at: state[2, :, at])
    enter(sy, lambda at: state[3, :, at])
    enter(sxy, lambda at: state[4, :, at])
    for copy in copies[1:]:
        copy.wait()
    enter(cp, lambda at: strength[:, at])
    enter(ca, lambda at: mass[:, at])
    enter(gx, lambda at: wind[0, :, at] + surface[0, :, at])
    enter(gy, lambda at: wind[1, :, at] + surface[1, :, at])

    lane = lane_index(pairs)
    final = (lane & (BX // 2 - 1)) == BX // 2 - 1
    initial = (lane & (BX // 2 - 1)) == 0

    def ahead(even, odd):
        return (
            odd - even,
            jnp.where(final, 0.0, pltpu.roll(even, LANES - 1, axis=1) - odd),
        )

    def behind(even, odd):
        return (
            even - jnp.where(initial, 0.0, pltpu.roll(odd, 1, axis=1)),
            odd - even,
        )

    def vec(odd, y):
        return pl.ds(odd * area + y * pairs, pairs)

    def row_of(ref, y):
        return (ref[vec(0, y), :], ref[vec(1, y), :])

    below = None
    for y in range(rows):
        p = tuple(RELAX * s for s in row_of(cp, y))
        across = behind(*p)
        for odd in range(2):
            i = vec(odd, y)
            m = ca[i, :]
            inverse = 1.0 / (m + SUB_STEP)
            push = SUB_STEP * inverse
            down = p[odd] if y == 0 else p[odd] - below[odd]
            gx[i, :] = push * (gx[i, :] - across[odd])
            gy[i, :] = push * (gy[i, :] - down)
            ca[i, :] = m * inverse
            cb[i, :] = push
            cq[i, :] = p[odd] * (0.625 * DECAY / 1.25**0.5)
            cp[i, :] = p[odd]
            sx[i, :] = sx[i, :] + p[odd]
            sy[i, :] = sy[i, :] + p[odd]
        below = p

    def sweep(step, carry):
        for _ in range(UNROLL):
            u, v = row_of(su, 0), row_of(sv, 0)
            above = None
            for y in range(rows):
                ux, vx = ahead(*u), ahead(*v)
                xx, yy, xy = [], [], []
                if y < rows - 1:
                    un, vn = row_of(su, y + 1), row_of(sv, y + 1)
                for odd in range(2):
                    i = vec(odd, y)
                    shear = vx[odd]
                    if y < rows - 1:
                        vy = vn[odd] - v[odd]
                        shear = shear + (un[odd] - u[odd])
                        a = ux[odd] + 0.6 * vy
                        b = 0.6 * ux[odd] + vy
                        d = ux[odd] * a + vy * b
                    else:
                        a = ux[odd]
                        b = 0.6 * a
                        d = a * a
                    small = 0.2 * shear
                    q = cq[i, :] * lax.rsqrt(d + (shear * small + 0.2))
                    xx.append(DECAY * sx[i, :] + q * a)
                    yy.append(DECAY * sy[i, :] + q * b)
                    xy.append(DECAY * sxy[i, :] + q * small)
                fx, fy = behind(*xx), behind(*xy)
                for odd in range(2):
                    i = vec(odd, y)
                    sx[i, :] = xx[odd]
                    sy[i, :] = yy[odd]
                    sxy[i, :] = xy[odd]
                    if y:
                        fxo = fx[odd] + (xy[odd] - above[0][odd])
                        fyo = fy[odd] + (yy[odd] - above[1][odd])
                    else:
                        fxo = fx[odd] + xy[odd]
                        fyo = fy[odd] + yy[odd]
                    a0 = ca[i, :]
                    b0 = cb[i, :]
                    uo, vo = u[odd], v[odd]
                    su[i, :] = a0 * (uo + TURNING * SUB_STEP * vo) + (b0 * fxo + gx[i, :])
                    sv[i, :] = a0 * (vo - TURNING * SUB_STEP * uo) + (b0 * fyo + gy[i, :])
                above = (xy, yy)
                if y < rows - 1:
                    u, v = un, vn
        return carry

    lax.fori_loop(0, SUBCYCLES // UNROLL, sweep, 0)

    sx[...] = sx[...] - cp[...]
    sy[...] = sy[...] - cp[...]
    for n, ref in enumerate((su, sv, sx, sy, sxy)):
        value = leave(ref)
        for b in range(blocks):
            at = slice(b * BX, (b + 1) * BX)
            new = value[(b // 2) * rows : (b // 2 + 1) * rows, (b % 2) * BX : (b % 2 + 1) * BX]
            keep = covered[b] == 1
            ice_out[n, :, at] = jnp.where(keep, new, state[n, :, at])
            if n < 2:
                part = fraction[:, at]
                w = wind[n, :, at]
                merged = part * (new - surface[n, :, at]) + (1.0 - part) * w
                stress_out[n, :, at] = jnp.where(keep, merged, w)


def ice(ice_state, strength, ice_mass, ice_fraction, wind_stress, ice_count, ice_list, ocean_state):
    rows, width = ice_mass.shape
    f32 = jnp.float32
    cells = (rows * width // BX, BX)
    return pl.pallas_call(
        ice_kernel,
        name="ice_subcycles",
        out_shape=(
            jax.ShapeDtypeStruct(ice_state.shape, f32),
            jax.ShapeDtypeStruct(wind_stress.shape, f32),
        ),
        in_specs=[spec(SMEM)] * 2 + [spec(HBM)] * 6,
        out_specs=(spec(VMEM), spec(VMEM)),
        scratch_shapes=[
            pltpu.VMEM((2 * BX, 2 * BX), jnp.bfloat16),
            pltpu.VMEM((2 * BX, 2 * BX), jnp.bfloat16),
            pltpu.VMEM(ice_state.shape, f32),
            pltpu.VMEM((rows, width), f32),
            pltpu.VMEM((rows, width), f32),
            pltpu.VMEM((rows, width), f32),
            pltpu.VMEM((2, rows, width), f32),
            pltpu.VMEM((2, rows, width), f32),
            pltpu.SemaphoreType.DMA((7,)),
            pltpu.SMEM((width // BX,), jnp.int32),
        ]
        + [pltpu.VMEM(cells, f32)] * 11,
        compiler_params=pltpu.CompilerParams(vmem_limit_bytes=VMEM_BYTES),
        cost_estimate=cost(SUBCYCLES * 50 * rows * width, 4 * 22 * rows * width),
    )(
        ice_count,
        ice_list,
        ice_state,
        strength,
        ice_mass,
        ice_fraction,
        wind_stress,
        ocean_state,
    )


def main_kernel(
    x_hbm,
    cols,
    bih,
    prev,
    cor,
    out_hbm,
    x,
    raw,
    out,
    y,
    matrix,
    in_sem,
    out_sem,
):
    fields, rows, levels, width = x.shape
    tiles = width // LANES

    def fetch(c):
        at = slice(c * LANES, (c + 1) * LANES)
        return pltpu.make_async_copy(x_hbm.at[:, :, at], raw.at[:, c], in_sem.at[c])

    def store(c):
        at = slice(c * LANES, (c + 1) * LANES)
        return pltpu.make_async_copy(out.at[:, c], out_hbm.at[:, :, at], out_sem.at[c])

    for c in range(tiles):
        fetch(c).start()
    make_columns(matrix)

    lane = lax.broadcasted_iota(jnp.int32, (rows * levels, LANES), 1)

    def tile(f, c):
        value = cols[f] if c < 0 or c >= tiles else x[f, :, :, c * LANES : (c + 1) * LANES]
        return value.reshape(rows * levels, LANES)

    def begin(c, f, slot):
        side = jnp.where(lane < LANES // 2, tile(f, c + 1), tile(f, c - 1))
        y[slot] = jnp.dot(
            jnp.concatenate(split(tile(f, c), 2) + split(side, 2), axis=1),
            matrix[...],
            preferred_element_type=jnp.float32,
        )

    def finish(c, f, slot):
        at = slice(c * LANES, (c + 1) * LANES)
        for r in range(rows):
            lap = y[slot, r * levels : (r + 1) * levels, 0:LANES]
            for step in (-1, 1):
                n = r + step
                if 0 <= n < rows:
                    lap = lap + y[slot, n * levels : (n + 1) * levels, LANES : 2 * LANES]
                if 0 <= n + step < rows:
                    lap = lap + x[f, n + step, :, at]
            out[f, c, pl.ds(r, levels, stride=rows), :] = lap
        for h in range(0, rows, HALF):
            hs = slice(h, h + HALF)
            coef = bih[hs, at]
            turn = cor[hs, :]
            before = here = raw[f, c, hs, :]
            for k in range(levels):
                ks = slice(k * rows + h, k * rows + h + HALF)
                if k + 1 < levels:
                    after = raw[f, c, (k + 1) * rows + h : (k + 1) * rows + h + HALF, :]
                else:
                    after = here
                res = (1.0 - 2.0 * KV_MIX) * here + KV_MIX * (before + after)
                res = res - coef * out[f, c, ks, :]
                if f == 0:
                    res = res + turn * raw[1, c, ks, :]
                elif f == 1:
                    res = res - turn * raw[0, c, ks, :]
                if f < 2 and k == 0:
                    res = res + prev[f, hs, at]
                out[f, c, ks, :] = res
                before, here = here, after
        if f == fields - 1:
            store(c).start()

    waited = 0
    pending = None
    for c in range(tiles):
        while waited < min(c + 2, tiles):
            fetch(waited).wait()
            to = slice(waited * LANES, (waited + 1) * LANES)
            for f in range(fields):
                for r in range(rows):
                    x[f, r, :, to] = raw[f, waited, pl.ds(r, levels, stride=rows), :]
            waited += 1
        for f in range(fields):
            job = (c, f, (c * fields + f) % 2)
            begin(*job)
            if pending is not None:
                finish(*pending)
            pending = job
    finish(*pending)
    for c in range(tiles):
        store(c).wait()


def ocean(ocean_state, cols, biharmonic, prev_stress, coriolis):
    fields, levels, rows, width = ocean_state.shape
    f32 = jnp.float32
    tiled = (fields, width // LANES, levels * rows, LANES)
    base = pl.pallas_call(
        main_kernel,
        name="ocean_tile",
        out_shape=jax.ShapeDtypeStruct((fields, levels * rows, width), f32),
        in_specs=[spec(HBM)] + [spec(VMEM)] * 4,
        out_specs=spec(HBM),
        scratch_shapes=[
            pltpu.VMEM((fields, rows, levels, width), f32),
            pltpu.VMEM(tiled, f32),
            pltpu.VMEM(tiled, f32),
            pltpu.VMEM((2, rows * levels, 2 * LANES), f32),
            pltpu.VMEM((4 * LANES, 2 * LANES), jnp.bfloat16),
            pltpu.SemaphoreType.DMA((width // LANES,)),
            pltpu.SemaphoreType.DMA((width // LANES,)),
        ],
        compiler_params=pltpu.CompilerParams(vmem_limit_bytes=VMEM_BYTES),
        cost_estimate=cost(30 * ocean_state.size, 8 * ocean_state.size),
    )(flatten(ocean_state), cols, biharmonic, prev_stress, coriolis)
    return base.reshape(ocean_state.shape)


def ends_kernel(above, below, out):
    width = above.shape[3]
    lane = lax.broadcasted_iota(jnp.int32, out.shape[2:], 1)
    for n, (halo, near) in enumerate(((above, 1), (below, 0))):
        for f in range(above.shape[1]):
            out[n, f] = jnp.where(
                lane < LANES // 2,
                halo[near, f, :, 0:LANES],
                halo[near, f, :, width - LANES : width],
            )


def ends(above, below):
    _, fields, levels, _ = above.shape
    return pl.pallas_call(
        ends_kernel,
        name="received_ends",
        out_shape=jax.ShapeDtypeStruct((2, fields, levels, LANES), jnp.float32),
        in_specs=[spec(VMEM)] * 2,
        out_specs=spec(VMEM),
        compiler_params=pltpu.CompilerParams(vmem_limit_bytes=SMALL_BYTES),
    )(above, below)


def fix_kernel(base, above, below, corners, bih, out, oa, ob, y, matrix, in_sem, out_sem):
    _, fields, levels, width = above.shape
    rows = base.shape[2]
    steps = width // WIDE
    fetches, stores = [], []
    for f in range(fields):
        mine, back = [], []
        for j in range(2):
            for side, (buf, first) in enumerate(((oa, 0), (ob, rows - 2))):
                n = (f * 2 + j) * 2 + side
                mine.append(
                    pltpu.make_async_copy(base.at[f, :, first + j, :], buf.at[f, j], in_sem.at[n])
                )
                back.append(
                    pltpu.make_async_copy(buf.at[f, j], out.at[f, :, first + j, :], out_sem.at[n])
                )
        fetches.append(mine)
        stores.append(back)
        for copy in mine:
            copy.start()

    make_columns(matrix)
    sides = ((above, 1), (below, 0))
    height = 2 * fields * levels
    lane = lax.broadcasted_iota(jnp.int32, (height, LANES), 1)

    def nearest(start, size):
        at = slice(start, start + size)
        return jnp.concatenate(
            [halo[near, f, :, at] for f in range(fields) for halo, near in sides], axis=0
        )

    ends = jnp.concatenate([corners[n, f] for f in range(fields) for n in range(2)], axis=0)
    for m in range(steps):
        west = ends if m == 0 else nearest(m * WIDE - LANES, LANES)
        east = ends if m == steps - 1 else nearest((m + 1) * WIDE, LANES)
        own = nearest(m * WIDE, WIDE)
        side = jnp.where(lane < LANES // 2, east, west)
        y[:, m * WIDE : (m + 1) * WIDE] = jnp.dot(
            jnp.concatenate(split(own, 2) + split(side, 2), axis=1),
            matrix[:, WIDE : 2 * WIDE],
            preferred_element_type=jnp.float32,
        )

    for f in range(fields):
        for copy in fetches[f]:
            copy.wait()
        for n, (halo, near, buf, n1, first) in enumerate(
            ((above, 1, oa, 0, 0), (below, 0, ob, 1, rows - 2))
        ):
            n2 = 1 - n1
            start = (2 * f + n) * levels
            for m in range(steps):
                at = slice(m * WIDE, (m + 1) * WIDE)
                lap = halo[1 - near, f, :, at] + y[start : start + levels, at]
                b1 = bih[first + n1 : first + n1 + 1, at]
                b2 = bih[first + n2 : first + n2 + 1, at]
                buf[f, n1, :, at] = buf[f, n1, :, at] - b1 * lap
                buf[f, n2, :, at] = buf[f, n2, :, at] - b2 * halo[near, f, :, at]
        for copy in stores[f]:
            copy.start()
    for back in stores:
        for copy in back:
            copy.wait()


def fix(base, above, below, corners, biharmonic):
    fields, levels, rows, width = base.shape
    f32 = jnp.float32
    edge = pltpu.VMEM((fields, 2, levels, width), f32)
    return pl.pallas_call(
        fix_kernel,
        name="ocean_edges",
        out_shape=jax.ShapeDtypeStruct(base.shape, f32),
        in_specs=[spec(HBM)] + [spec(VMEM)] * 4,
        out_specs=spec(HBM),
        input_output_aliases={0: 0},
        scratch_shapes=[
            edge,
            edge,
            pltpu.VMEM((2 * fields * levels, width), f32),
            pltpu.VMEM((2 * (WIDE + LANES), 2 * WIDE), jnp.bfloat16),
            pltpu.SemaphoreType.DMA((4 * fields,)),
            pltpu.SemaphoreType.DMA((4 * fields,)),
        ],
        compiler_params=pltpu.CompilerParams(vmem_limit_bytes=SMALL_BYTES),
        cost_estimate=cost(0, 3 * 4 * 4 * fields * levels * width),
    )(base, above, below, corners, biharmonic)


def per_device(
    ocean_state,
    biharmonic,
    prev_stress,
    ice_state,
    strength,
    ice_mass,
    ice_fraction,
    wind_stress,
    ice_count,
    ice_list,
):
    tile_rows = ocean_state.shape[2]
    n_tile = lax.axis_size("tile")
    n_grp = lax.axis_size("grp")

    first, last, cols = pack(ocean_state)

    def shift(value, tile_step, grp_step):
        pairs = []
        for g in range(n_grp):
            for t in range(n_tile):
                if 0 <= t + tile_step < n_tile:
                    target = (g + grp_step) % n_grp
                    pairs.append((g * n_tile + t, target * n_tile + t + tile_step))
        return lax.ppermute(value, ("grp", "tile"), pairs)

    def around(value):
        west = shift(value, 0, 1)
        if n_grp == 2:
            return west
        return jnp.where(jnp.arange(LANES) < LANES // 2, shift(value, 0, -1), west)

    above = shift(last, 1, 0)
    below = shift(first, -1, 0)
    cols = around(cols)

    ice_in = (ice_state, strength, ice_mass, ice_fraction, wind_stress, ice_count, ice_list)
    ice_out, stress_out = ice(*ice_in, ocean_state)

    rows = (lax.axis_index("tile") * tile_rows + jnp.arange(tile_rows)).astype(jnp.float32) + 0.5
    coriolis = CORIOLIS * (2.0 * rows / (tile_rows * n_tile) - 1.0)
    coriolis = jnp.broadcast_to(coriolis[:, None], (tile_rows, LANES))

    cols, ice_out, stress_out = lax.optimization_barrier((cols, ice_out, stress_out))
    base = ocean(ocean_state, cols, biharmonic, prev_stress, coriolis)

    above, below, base = lax.optimization_barrier((above, below, base))
    corners = around(ends(above, below))
    ocean_out = fix(base, above, below, corners, biharmonic)
    return (ocean_out, ice_out, stress_out)


def solution(mesh):
    placed = (
        P(None, None, "tile", "grp"),
        P("tile", "grp"),
        P(None, "tile", "grp"),
        P(None, "tile", "grp"),
        P("tile", "grp"),
        P("tile", "grp"),
        P("tile", "grp"),
        P(None, "tile", "grp"),
        P(("grp", "tile")),
        P(("grp", "tile"), None),
    )
    return jax.shard_map(
        per_device,
        mesh=mesh,
        in_specs=placed,
        out_specs=(P(None, None, "tile", "grp"), P(None, "tile", "grp"), P(None, "tile", "grp")),
        check_vma=False,
    )
```

```python
import jax
import jax.numpy as jnp
from jax import lax
from jax.experimental import pallas as pl
from jax.experimental.pallas import tpu as pltpu
from jax.sharding import PartitionSpec as P

BY = 16
BX = 128
SUBCYCLES = 64
UNROLL = 4
LANES = 128
HALF = 8

KV_MIX = 0.2
RELAX = 0.5
SUB_STEP = 0.3
TURNING = 0.3
CORIOLIS = 0.2

DECAY = 1.0 / (1.0 + RELAX)
VMEM_BYTES = 48 * 1024 * 1024
SMALL_BYTES = 24 * 1024 * 1024

HBM = pltpu.HBM
VMEM = pltpu.VMEM
SMEM = pltpu.SMEM


def spec(space):
    return pl.BlockSpec(memory_space=space)


def cost(flops, nbytes):
    return pl.CostEstimate(flops=flops, bytes_accessed=nbytes, transcendentals=0)


def lane_index(rows):
    return lax.broadcasted_iota(jnp.int32, (rows, LANES), 1)


WIDE = 256


def iota(shape, dim):
    return lax.broadcasted_iota(jnp.int32, shape, dim)


def as_matrix(value):
    return value.astype(jnp.float32).astype(jnp.bfloat16)


def column_taps(source, shape):
    place = iota(shape, 1)
    wide = shape[1] // 2
    d = jnp.abs(source - (place & (wide - 1)))
    double = jnp.where(d == 0, 20, jnp.where(d == 1, -8, jnp.where(d == 2, 1, 0)))
    single = jnp.where(d == 0, -8, jnp.where(d == 1, 2, 0))
    return as_matrix(jnp.where(place < wide, double, single))


def make_columns(matrix):
    wide = matrix.shape[1] // 2
    own = (wide, 2 * wide)
    taps = column_taps(iota(own, 0), own)
    matrix[0:wide, :] = taps
    matrix[wide : 2 * wide, :] = taps
    side = (LANES, 2 * wide)
    lane = iota(side, 0)
    taps = column_taps(jnp.where(lane < LANES // 2, lane + wide, lane - LANES), side)
    matrix[2 * wide : 2 * wide + LANES, :] = taps
    matrix[2 * wide + LANES : 2 * wide + 2 * LANES, :] = taps


def make_orders(forward, backward):
    shape = forward.shape

    def target(i):
        return ((i & 1) * BX) + ((i >> 7) * (BX // 2)) + ((i & (BX - 1)) >> 1)

    forward[...] = as_matrix(jnp.where(target(iota(shape, 0)) == iota(shape, 1), 1, 0))
    backward[...] = as_matrix(jnp.where(target(iota(shape, 1)) == iota(shape, 0), 1, 0))


def pack_kernel(
    x,
    flat,
    first,
    last,
    cols,
    left,
    right,
    row_sem,
    col_sem,
):
    rows, width = x.shape[2:]
    copies = []
    for j in range(2):
        for side, (to, row) in enumerate(((first, j), (last, rows - 2 + j))):
            copies.append(
                pltpu.make_async_copy(x.at[:, :, row, :], to.at[j], row_sem.at[side, j])
            )
    col_copies = [
        pltpu.make_async_copy(flat.at[:, :, start : start + LANES], to, col_sem.at[side])
        for side, (to, start) in enumerate(((left, 0), (right, width - LANES)))
    ]
    for copy in copies + col_copies:
        copy.start()
    for copy in col_copies:
        copy.wait()
    lane = lax.broadcasted_iota(jnp.int32, cols.shape[2:], 1)
    levels = x.shape[1]
    for f in range(left.shape[0]):
        for r in range(rows):
            at = pl.ds(r, levels, stride=rows)
            cols[f, r] = jnp.where(lane < LANES // 2, left[f, at, :], right[f, at, :])
    for copy in copies:
        copy.wait()


def flatten(array):
    fields, levels, rows, width = array.shape
    return array.reshape(fields, levels * rows, width)


def pack(ocean_state):
    fields, levels, rows, width = ocean_state.shape
    f32 = jnp.float32
    edge = (fields, rows, levels, LANES)
    return pl.pallas_call(
        pack_kernel,
        name="pack_edges",
        out_shape=(
            jax.ShapeDtypeStruct((2, fields, levels, width), f32),
            jax.ShapeDtypeStruct((2, fields, levels, width), f32),
            jax.ShapeDtypeStruct(edge, f32),
        ),
        in_specs=[spec(HBM)] * 2,
        out_specs=(spec(VMEM),) * 3,
        scratch_shapes=[
            pltpu.VMEM((fields, levels * rows, LANES), f32),
            pltpu.VMEM((fields, levels * rows, LANES), f32),
            pltpu.SemaphoreType.DMA((2, 2)),
            pltpu.SemaphoreType.DMA((2,)),
        ],
        compiler_params=pltpu.CompilerParams(vmem_limit_bytes=VMEM_BYTES),
        cost_estimate=cost(0, 4 * 2 * 4 * fields * levels * width),
    )(ocean_state, flatten(ocean_state))


def split(q, parts):
    out = []
    for _ in range(parts):
        part = q.astype(jnp.bfloat16)
        out.append(part)
        q = q - part.astype(jnp.float32)
    return out


def reorder(value, matrix):
    total = None
    for part in split(value, 3):
        term = jnp.dot(part, matrix, preferred_element_type=jnp.float32)
        total = term if total is None else total + term
    return total


def ice_kernel(
    count,
    listed,
    state_hbm,
    strength_hbm,
    mass_hbm,
    fraction_hbm,
    wind_hbm,
    ocean_hbm,
    ice_out,
    stress_out,
    forward,
    backward,
    state,
    strength,
    mass,
    fraction,
    wind,
    surface,
    sem,
    covered,
    su,
    sv,
    sx,
    sy,
    sxy,
    cp,
    cq,
    ca,
    cb,
    gx,
    gy,
):
    rows, width = mass.shape
    wide = 2 * BX
    pairs = width // wide
    area = rows * pairs
    blocks = width // BX

    copies = [
        pltpu.make_async_copy(source, to, sem.at[n])
        for n, (source, to) in enumerate(
            (
                (state_hbm, state),
                (strength_hbm, strength),
                (mass_hbm, mass),
                (wind_hbm, wind),
                (ocean_hbm.at[0, 0], surface.at[0]),
                (ocean_hbm.at[1, 0], surface.at[1]),
                (fraction_hbm, fraction),
            )
        )
    ]
    for copy in copies:
        copy.start()

    make_orders(forward, backward)
    for s in range(blocks):
        covered[listed[0, s]] = jnp.where(s < count[0], 1, 0)

    def chunk(j):
        return slice(j * wide, (j + 1) * wide)

    def place(j, odd):
        return pl.ds(odd * area + j, rows, stride=pairs)

    def enter(ref, get):
        value = jnp.concatenate([get(chunk(j)) for j in range(pairs)], axis=0)
        value = reorder(value, forward[...])
        for j in range(pairs):
            for odd in range(2):
                ref[place(j, odd), :] = value[
                    j * rows : (j + 1) * rows, odd * BX : (odd + 1) * BX
                ]

    def leave(ref):
        value = jnp.concatenate(
            [
                jnp.concatenate([ref[place(j, 0), :], ref[place(j, 1), :]], axis=1)
                for j in range(pairs)
            ],
            axis=0,
        )
        return reorder(value, backward[...])

    copies[0].wait()
    enter(su, lambda at: state[0, :, at])
    enter(sv, lambda at: state[1, :, at])
    enter(sx, lambda at: state[2, :, at])
    enter(sy, lambda at: state[3, :, at])
    enter(sxy, lambda at: state[4, :, at])
    for copy in copies[1:]:
        copy.wait()
    enter(cp, lambda at: strength[:, at])
    enter(ca, lambda at: mass[:, at])
    enter(gx, lambda at: wind[0, :, at] + surface[0, :, at])
    enter(gy, lambda at: wind[1, :, at] + surface[1, :, at])

    lane = lane_index(pairs)
    final = (lane & (BX // 2 - 1)) == BX // 2 - 1
    initial = (lane & (BX // 2 - 1)) == 0

    def ahead(even, odd):
        return (
            odd - even,
            jnp.where(final, 0.0, pltpu.roll(even, LANES - 1, axis=1) - odd),
        )

    def behind(even, odd):
        return (
            even - jnp.where(initial, 0.0, pltpu.roll(odd, 1, axis=1)),
            odd - even,
        )

    def vec(odd, y):
        return pl.ds(odd * area + y * pairs, pairs)

    def row_of(ref, y):
        return (ref[vec(0, y), :], ref[vec(1, y), :])

    below = None
    for y in range(rows):
        p = tuple(RELAX * s for s in row_of(cp, y))
        across = behind(*p)
        for odd in range(2):
            i = vec(odd, y)
            m = ca[i, :]
            inverse = 1.0 / (m + SUB_STEP)
            push = SUB_STEP * inverse
            down = p[odd] if y == 0 else p[odd] - below[odd]
            gx[i, :] = push * (gx[i, :] - across[odd])
            gy[i, :] = push * (gy[i, :] - down)
            ca[i, :] = m * inverse
            cb[i, :] = push
            cq[i, :] = p[odd] * (0.625 * DECAY / 1.25**0.5)
            cp[i, :] = p[odd]
            sx[i, :] = sx[i, :] + p[odd]
            sy[i, :] = sy[i, :] + p[odd]
        below = p

    def sweep(step, carry):
        for _ in range(UNROLL):
            u, v = row_of(su, 0), row_of(sv, 0)
            above = None
            for y in range(rows):
                ux, vx = ahead(*u), ahead(*v)
                xx, yy, xy = [], [], []
                if y < rows - 1:
                    un, vn = row_of(su, y + 1), row_of(sv, y + 1)
                for odd in range(2):
                    i = vec(odd, y)
                    shear = vx[odd]
                    if y < rows - 1:
                        vy = vn[odd] - v[odd]
                        shear = shear + (un[odd] - u[odd])
                        a = ux[odd] + 0.6 * vy
                        b = 0.6 * ux[odd] + vy
                        d = ux[odd] * a + vy * b
                    else:
                        a = ux[odd]
                        b = 0.6 * a
                        d = a * a
                    small = 0.2 * shear
                    q = cq[i, :] * lax.rsqrt(d + (shear * small + 0.2))
                    xx.append(DECAY * sx[i, :] + q * a)
                    yy.append(DECAY * sy[i, :] + q * b)
                    xy.append(DECAY * sxy[i, :] + q * small)
                fx, fy = behind(*xx), behind(*xy)
                for odd in range(2):
                    i = vec(odd, y)
                    sx[i, :] = xx[odd]
                    sy[i, :] = yy[odd]
                    sxy[i, :] = xy[odd]
                    if y:
                        fxo = fx[odd] + (xy[odd] - above[0][odd])
                        fyo = fy[odd] + (yy[odd] - above[1][odd])
                    else:
                        fxo = fx[odd] + xy[odd]
                        fyo = fy[odd] + yy[odd]
                    a0 = ca[i, :]
                    b0 = cb[i, :]
                    uo, vo = u[odd], v[odd]
                    su[i, :] = a0 * (uo + TURNING * SUB_STEP * vo) + (b0 * fxo + gx[i, :])
                    sv[i, :] = a0 * (vo - TURNING * SUB_STEP * uo) + (b0 * fyo + gy[i, :])
                above = (xy, yy)
                if y < rows - 1:
                    u, v = un, vn
        return carry

    lax.fori_loop(0, SUBCYCLES // UNROLL, sweep, 0)

    sx[...] = sx[...] - cp[...]
    sy[...] = sy[...] - cp[...]
    for n, ref in enumerate((su, sv, sx, sy, sxy)):
        value = leave(ref)
        for b in range(blocks):
            at = slice(b * BX, (b + 1) * BX)
            new = value[(b // 2) * rows : (b // 2 + 1) * rows, (b % 2) * BX : (b % 2 + 1) * BX]
            keep = covered[b] == 1
            ice_out[n, :, at] = jnp.where(keep, new, state[n, :, at])
            if n < 2:
                part = fraction[:, at]
                w = wind[n, :, at]
                merged = part * (new - surface[n, :, at]) + (1.0 - part) * w
                stress_out[n, :, at] = jnp.where(keep, merged, w)


def ice(ice_state, strength, ice_mass, ice_fraction, wind_stress, ice_count, ice_list, ocean_state):
    rows, width = ice_mass.shape
    f32 = jnp.float32
    cells = (rows * width // BX, BX)
    return pl.pallas_call(
        ice_kernel,
        name="ice_subcycles",
        out_shape=(
            jax.ShapeDtypeStruct(ice_state.shape, f32),
            jax.ShapeDtypeStruct(wind_stress.shape, f32),
        ),
        in_specs=[spec(SMEM)] * 2 + [spec(HBM)] * 6,
        out_specs=(spec(VMEM), spec(VMEM)),
        scratch_shapes=[
            pltpu.VMEM((2 * BX, 2 * BX), jnp.bfloat16),
            pltpu.VMEM((2 * BX, 2 * BX), jnp.bfloat16),
            pltpu.VMEM(ice_state.shape, f32),
            pltpu.VMEM((rows, width), f32),
            pltpu.VMEM((rows, width), f32),
            pltpu.VMEM((rows, width), f32),
            pltpu.VMEM((2, rows, width), f32),
            pltpu.VMEM((2, rows, width), f32),
            pltpu.SemaphoreType.DMA((7,)),
            pltpu.SMEM((width // BX,), jnp.int32),
        ]
        + [pltpu.VMEM(cells, f32)] * 11,
        compiler_params=pltpu.CompilerParams(vmem_limit_bytes=VMEM_BYTES),
        cost_estimate=cost(SUBCYCLES * 50 * rows * width, 4 * 22 * rows * width),
    )(
        ice_count,
        ice_list,
        ice_state,
        strength,
        ice_mass,
        ice_fraction,
        wind_stress,
        ocean_state,
    )


def main_kernel(
    x_hbm,
    cols,
    bih,
    prev,
    cor,
    out_hbm,
    x,
    raw,
    out,
    y,
    matrix,
    in_sem,
    out_sem,
):
    fields, rows, levels, width = x.shape
    tiles = width // LANES - 1

    def lanes(c):
        start = c * LANES
        return pl.ds(start if isinstance(c, int) else pl.multiple_of(start, LANES), LANES)

    def fetch(c):
        at = lanes(c)
        return pltpu.make_async_copy(x_hbm.at[:, :, at], raw.at[:, c], in_sem.at[c])

    def store(c):
        at = lanes(c)
        return pltpu.make_async_copy(out.at[:, c], out_hbm.at[:, :, at], out_sem.at[c])

    for c in range(tiles):
        fetch(c).start()
    make_columns(matrix)
    x[:, :, :, lanes(tiles)] = cols[...]

    lane = lax.broadcasted_iota(jnp.int32, (rows * levels, LANES), 1)

    def tile(f, c):
        return x[f, :, :, lanes(c)].reshape(rows * levels, LANES)

    def begin(c, f, slot):
        west = jnp.where(c == 0, tiles, c - 1)
        side = jnp.where(lane < LANES // 2, tile(f, c + 1), tile(f, west))
        y[slot] = jnp.dot(
            jnp.concatenate(split(tile(f, c), 2) + split(side, 2), axis=1),
            matrix[...],
            preferred_element_type=jnp.float32,
        )

    def finish(c, f, slot):
        at = lanes(c)
        for r in range(rows):
            lap = y[slot, r * levels : (r + 1) * levels, 0:LANES]
            for step in (-1, 1):
                n = r + step
                if 0 <= n < rows:
                    lap = lap + y[slot, n * levels : (n + 1) * levels, LANES : 2 * LANES]
                if 0 <= n + step < rows:
                    lap = lap + x[f, n + step, :, at]
            out[f, c, pl.ds(r, levels, stride=rows), :] = lap
        for h in range(0, rows, HALF):
            hs = slice(h, h + HALF)
            coef = bih[hs, at]
            turn = cor[hs, :]
            before = here = raw[f, c, hs, :]
            for k in range(levels):
                ks = slice(k * rows + h, k * rows + h + HALF)
                if k + 1 < levels:
                    after = raw[f, c, (k + 1) * rows + h : (k + 1) * rows + h + HALF, :]
                else:
                    after = here
                res = (1.0 - 2.0 * KV_MIX) * here + KV_MIX * (before + after)
                res = res - coef * out[f, c, ks, :]
                if f == 0:
                    res = res + turn * raw[1, c, ks, :]
                elif f == 1:
                    res = res - turn * raw[0, c, ks, :]
                if f < 2 and k == 0:
                    res = res + prev[f, hs, at]
                out[f, c, ks, :] = res
                before, here = here, after
    def turn_rows(c):
        fetch(c).wait()
        for f in range(fields):
            for r in range(rows):
                x[f, r, :, lanes(c)] = raw[f, c, pl.ds(r, levels, stride=rows), :]

    turn_rows(0)

    def column(c, carry):
        @pl.when(c + 1 < tiles)
        def _():
            turn_rows(c + 1)

        begin(c, 0, 0)
        for f in range(fields):
            if f + 1 < fields:
                begin(c, f + 1, f + 1)
            finish(c, f, f)
        store(c).start()
        return carry

    lax.fori_loop(0, tiles, column, 0)
    for c in range(tiles):
        store(c).wait()


def ocean(ocean_state, cols, biharmonic, prev_stress, coriolis):
    fields, levels, rows, width = ocean_state.shape
    f32 = jnp.float32
    tiled = (fields, width // LANES, levels * rows, LANES)
    base = pl.pallas_call(
        main_kernel,
        name="ocean_tile",
        out_shape=jax.ShapeDtypeStruct((fields, levels * rows, width), f32),
        in_specs=[spec(HBM)] + [spec(VMEM)] * 4,
        out_specs=spec(HBM),
        scratch_shapes=[
            pltpu.VMEM((fields, rows, levels, width + LANES), f32),
            pltpu.VMEM(tiled, f32),
            pltpu.VMEM(tiled, f32),
            pltpu.VMEM((fields, rows * levels, 2 * LANES), f32),
            pltpu.VMEM((4 * LANES, 2 * LANES), jnp.bfloat16),
            pltpu.SemaphoreType.DMA((width // LANES,)),
            pltpu.SemaphoreType.DMA((width // LANES,)),
        ],
        compiler_params=pltpu.CompilerParams(vmem_limit_bytes=VMEM_BYTES),
        cost_estimate=cost(30 * ocean_state.size, 8 * ocean_state.size),
    )(flatten(ocean_state), cols, biharmonic, prev_stress, coriolis)
    return base.reshape(ocean_state.shape)


def ends_kernel(above, below, out):
    width = above.shape[3]
    lane = lax.broadcasted_iota(jnp.int32, out.shape[2:], 1)
    for n, (halo, near) in enumerate(((above, 1), (below, 0))):
        for f in range(above.shape[1]):
            out[n, f] = jnp.where(
                lane < LANES // 2,
                halo[near, f, :, 0:LANES],
                halo[near, f, :, width - LANES : width],
            )


def ends(above, below):
    _, fields, levels, _ = above.shape
    return pl.pallas_call(
        ends_kernel,
        name="received_ends",
        out_shape=jax.ShapeDtypeStruct((2, fields, levels, LANES), jnp.float32),
        in_specs=[spec(VMEM)] * 2,
        out_specs=spec(VMEM),
        compiler_params=pltpu.CompilerParams(vmem_limit_bytes=SMALL_BYTES),
    )(above, below)


def fix_kernel(base, above, below, corners, bih, out, oa, ob, y, matrix, in_sem, out_sem):
    _, fields, levels, width = above.shape
    rows = base.shape[2]
    steps = width // WIDE
    fetches, stores = [], []
    for f in range(fields):
        mine, back = [], []
        for j in range(2):
            for side, (buf, first) in enumerate(((oa, 0), (ob, rows - 2))):
                n = (f * 2 + j) * 2 + side
                mine.append(
                    pltpu.make_async_copy(base.at[f, :, first + j, :], buf.at[f, j], in_sem.at[n])
                )
                back.append(
                    pltpu.make_async_copy(buf.at[f, j], out.at[f, :, first + j, :], out_sem.at[n])
                )
        fetches.append(mine)
        stores.append(back)
        for copy in mine:
            copy.start()

    make_columns(matrix)
    sides = ((above, 1), (below, 0))
    height = 2 * fields * levels
    lane = lax.broadcasted_iota(jnp.int32, (height, LANES), 1)

    def nearest(start, size):
        at = slice(start, start + size)
        return jnp.concatenate(
            [halo[near, f, :, at] for f in range(fields) for halo, near in sides], axis=0
        )

    ends = jnp.concatenate([corners[n, f] for f in range(fields) for n in range(2)], axis=0)
    for m in range(steps):
        west = ends if m == 0 else nearest(m * WIDE - LANES, LANES)
        east = ends if m == steps - 1 else nearest((m + 1) * WIDE, LANES)
        own = nearest(m * WIDE, WIDE)
        side = jnp.where(lane < LANES // 2, east, west)
        y[:, m * WIDE : (m + 1) * WIDE] = jnp.dot(
            jnp.concatenate(split(own, 2) + split(side, 2), axis=1),
            matrix[:, WIDE : 2 * WIDE],
            preferred_element_type=jnp.float32,
        )

    for f in range(fields):
        for copy in fetches[f]:
            copy.wait()
        for n, (halo, near, buf, n1, first) in enumerate(
            ((above, 1, oa, 0, 0), (below, 0, ob, 1, rows - 2))
        ):
            n2 = 1 - n1
            start = (2 * f + n) * levels
            for m in range(steps):
                at = slice(m * WIDE, (m + 1) * WIDE)
                lap = halo[1 - near, f, :, at] + y[start : start + levels, at]
                b1 = bih[first + n1 : first + n1 + 1, at]
                b2 = bih[first + n2 : first + n2 + 1, at]
                buf[f, n1, :, at] = buf[f, n1, :, at] - b1 * lap
                buf[f, n2, :, at] = buf[f, n2, :, at] - b2 * halo[near, f, :, at]
        for copy in stores[f]:
            copy.start()
    for back in stores:
        for copy in back:
            copy.wait()


def fix(base, above, below, corners, biharmonic):
    fields, levels, rows, width = base.shape
    f32 = jnp.float32
    edge = pltpu.VMEM((fields, 2, levels, width), f32)
    return pl.pallas_call(
        fix_kernel,
        name="ocean_edges",
        out_shape=jax.ShapeDtypeStruct(base.shape, f32),
        in_specs=[spec(HBM)] + [spec(VMEM)] * 4,
        out_specs=spec(HBM),
        input_output_aliases={0: 0},
        scratch_shapes=[
            edge,
            edge,
            pltpu.VMEM((2 * fields * levels, width), f32),
            pltpu.VMEM((2 * (WIDE + LANES), 2 * WIDE), jnp.bfloat16),
            pltpu.SemaphoreType.DMA((4 * fields,)),
            pltpu.SemaphoreType.DMA((4 * fields,)),
        ],
        compiler_params=pltpu.CompilerParams(vmem_limit_bytes=SMALL_BYTES),
        cost_estimate=cost(0, 3 * 4 * 4 * fields * levels * width),
    )(base, above, below, corners, biharmonic)


def per_device(
    ocean_state,
    biharmonic,
    prev_stress,
    ice_state,
    strength,
    ice_mass,
    ice_fraction,
    wind_stress,
    ice_count,
    ice_list,
):
    tile_rows = ocean_state.shape[2]
    n_tile = lax.axis_size("tile")
    n_grp = lax.axis_size("grp")

    first, last, cols = pack(ocean_state)

    def shift(value, tile_step, grp_step):
        pairs = []
        for g in range(n_grp):
            for t in range(n_tile):
                if 0 <= t + tile_step < n_tile:
                    target = (g + grp_step) % n_grp
                    pairs.append((g * n_tile + t, target * n_tile + t + tile_step))
        return lax.ppermute(value, ("grp", "tile"), pairs)

    def around(value):
        west = shift(value, 0, 1)
        if n_grp == 2:
            return west
        return jnp.where(jnp.arange(LANES) < LANES // 2, shift(value, 0, -1), west)

    above = shift(last, 1, 0)
    below = shift(first, -1, 0)
    cols = around(cols)

    ice_in = (ice_state, strength, ice_mass, ice_fraction, wind_stress, ice_count, ice_list)
    ice_out, stress_out = ice(*ice_in, ocean_state)

    rows = (lax.axis_index("tile") * tile_rows + jnp.arange(tile_rows)).astype(jnp.float32) + 0.5
    coriolis = CORIOLIS * (2.0 * rows / (tile_rows * n_tile) - 1.0)
    coriolis = jnp.broadcast_to(coriolis[:, None], (tile_rows, LANES))

    cols, ice_out, stress_out = lax.optimization_barrier((cols, ice_out, stress_out))
    base = ocean(ocean_state, cols, biharmonic, prev_stress, coriolis)

    above, below, base = lax.optimization_barrier((above, below, base))
    corners = around(ends(above, below))
    ocean_out = fix(base, above, below, corners, biharmonic)
    return (ocean_out, ice_out, stress_out)


def solution(mesh):
    placed = (
        P(None, None, "tile", "grp"),
        P("tile", "grp"),
        P(None, "tile", "grp"),
        P(None, "tile", "grp"),
        P("tile", "grp"),
        P("tile", "grp"),
        P("tile", "grp"),
        P(None, "tile", "grp"),
        P(("grp", "tile")),
        P(("grp", "tile"), None),
    )
    return jax.shard_map(
        per_device,
        mesh=mesh,
        in_specs=placed,
        out_specs=(P(None, None, "tile", "grp"), P(None, "tile", "grp"), P(None, "tile", "grp")),
        check_vma=False,
    )
```
